128 devices in a mesh: lon: 16 (over z_lo, x, core), lat: 8 (over y, z_hi).
Axes of the slice: x: 4, y: 4, z: 4 (z_hi: 2, z_lo: 2; z = z_hi * 2 + z_lo), core: 2. Of those that a mesh axis runs over, the one named last changes fastest.
Arguments:
- trajectory: float32 [3, 32, 512, 2048], P(None, None, 'lat', 'lon'), may hold values from -6 to 6
- adjoint_in: float32 [3, 32, 512, 2048], P(None, None, 'lat', 'lon'), may hold values from -6 to 6
- cutoffs: int32 [2, 64], replicated, may hold values from 2 to 511
Outputs:
- adjoint_out: float32 [3, 32, 512, 2048], P(None, None, 'lat', 'lon')
The draws below stay inside these ranges and needn't reach their ends.
All inputs are finite; a program needn't handle non-finite values.
Results may differ from the reference program's by a relative error of at most 0.0003.
Values sent between devices are 32-bit elements; how exact they have to be, the bound alone decides.
A program may use at most 128 MiB of HBM per device.

```python
import jax
import jax.numpy as jnp
from jax import lax

NLON = 2048
LEV = 32
LAT_DEV = 64
NLAT = 512


def plant(array, rng, least, largest):
    spot = [jax.random.randint(jax.random.fold_in(rng, axis), (), 0, length) for axis, length in enumerate(array.shape)]
    widest = array.shape.index(max(array.shape))
    beside = spot[:widest] + [(spot[widest] + 1) % array.shape[widest]] + spot[widest + 1:]
    return array.at[tuple(spot)].set(least).at[tuple(beside)].set(largest)


def shard_levels(own_key, shape, cuts, least, high):
    def one(dim, shards_of):
        heights = jax.random.uniform(jax.random.fold_in(jax.random.fold_in(own_key, 6), dim), (shards_of,), jnp.float32, least / len(cuts), high / len(cuts))
        return jnp.repeat(jnp.exp(heights), shape[dim] // shards_of).reshape((-1,) + (1,) * (len(shape) - dim - 1))

    factor_of = one(*cuts[0])
    for cut in cuts[1:]:
        factor_of = factor_of * one(*cut)
    return factor_of


def gaussian(own_key, dims, spread, most, split=(), kind=jnp.bfloat16):
    gain = shard_levels(own_key, dims, split, -0.22, 0.18) if split else 1.0
    values = jax.random.normal(own_key, dims, jnp.float32) * spread * gain
    return jnp.minimum(jnp.maximum(values, -most), most).astype(kind)


def setup_inputs(seed: int = 0) -> dict:
    seeds = jax.random.split(jax.random.key(seed), 4)
    trajectory = gaussian(seeds[0], (3, LEV, NLAT, NLON), 1.0, 6.0, ((2, 8), (3, 16)), jnp.float32)
    adjoint_in = gaussian(seeds[1], (3, LEV, NLAT, NLON), 1.0, 6.0, ((2, 8), (3, 16)), jnp.float32)
    cutoffs = plant(jax.random.randint(seeds[2], (2, LAT_DEV), 2, NLON // 4), jax.random.fold_in(seeds[2], 1), 2, (NLON // 4) - 1).astype(jnp.int32)
    return dict(trajectory=trajectory, adjoint_in=adjoint_in, cutoffs=cutoffs)


cx = 0.25
cy = 0.25
cg = 0.3
ca = 0.25

def out_region(delta, state, rows, nlat):
    h_in, u_in, v_in = (delta[0], delta[1], delta[2])
    h_st, u_st, v_st = (state[0], state[1], state[2])
    east_u = 0.5 * (u_st[:, :, :-1] + u_st[:, :, 1:])
    east_h = 0.5 * (h_st[:, :, :-1] + h_st[:, :, 1:])
    flux_x = east_u * 0.5 * (h_in[:, :, :-1] + h_in[:, :, 1:]) + east_h * 0.5 * (u_in[:, :, :-1] + u_in[:, :, 1:])
    valid = ((rows[:-1] >= 0) & (rows[1:] <= nlat - 1)).astype(jnp.float32)[None, :, None]
    north_v = 0.5 * (v_st[:, :-1, :] + v_st[:, 1:, :])
    north_h = 0.5 * (h_st[:, :-1, :] + h_st[:, 1:, :])
    flux_y = valid * (north_v * 0.5 * (h_in[:, :-1, :] + h_in[:, 1:, :]) + north_h * 0.5 * (v_in[:, :-1, :] + v_in[:, 1:, :]))
    div_x = flux_x[:, 1:-1, 1:] - flux_x[:, 1:-1, :-1]
    div_y = flux_y[:, 1:, 1:-1] - flux_y[:, :-1, 1:-1]
    h_out = h_in[:, 1:-1, 1:-1] - cx * div_x - cy * div_y
    u_out = u_in[:, 1:-1, 1:-1] - cg * (h_in[:, 1:-1, 2:] - h_in[:, 1:-1, :-2]) - ca * u_st[:, 1:-1, 1:-1] * (u_in[:, 1:-1, 2:] - u_in[:, 1:-1, :-2])
    v_out = v_in[:, 1:-1, 1:-1] - cg * (h_in[:, 2:, 1:-1] - h_in[:, :-2, 1:-1]) - ca * v_st[:, 1:-1, 1:-1] * (v_in[:, 2:, 1:-1] - v_in[:, :-2, 1:-1])
    return jnp.stack([h_out, u_out, v_out], 0)

def fourier_columns(nlon, start, width):
    index = jnp.arange(nlon, dtype=jnp.int32)[:, None]
    column = start + jnp.arange(width, dtype=jnp.int32)[None, :]
    half = nlon // 2
    wave = jnp.where(column <= half, column, column - half)
    phase = index * wave % nlon
    angle = 2.0 * jnp.pi / nlon * phase.astype(jnp.float32)
    scale = jnp.sqrt(2.0 / nlon)
    table = jnp.where(column == 0, 1.0 / jnp.sqrt(1.0 * nlon), jnp.where(column == half, jnp.cos(angle) / jnp.sqrt(1.0 * nlon), jnp.where(column < half, scale * jnp.cos(angle), scale * jnp.sin(angle))))
    return (table.astype(jnp.float32), wave[0].astype(jnp.float32))

def filter_rows(rows, cut):
    nlon = rows.shape[1]
    table, wave = fourier_columns(nlon, 0, nlon)
    spectrum = jnp.dot(rows, table, precision=lax.Precision.HIGHEST)
    damp = jnp.minimum(1.0, (cut[:, None] / jnp.maximum(wave, 1.0)[None, :]) ** 2)
    return lax.dot_general(spectrum * damp, table, (((1,), (1,)), ((), ())), precision=lax.Precision.HIGHEST)

def pad_field(field):
    wrapped = jnp.pad(field, ((0, 0), (0, 0), (0, 0), (1, 1)), mode='wrap')
    return jnp.pad(wrapped, ((0, 0), (0, 0), (1, 1), (0, 0)))

def reference(trajectory, adjoint_in, cutoffs):
    fields, levels, nlat, nlon = adjoint_in.shape
    cap = cutoffs.shape[1]
    count = fields * levels * cap
    row_cap = jnp.arange(count, dtype=jnp.int32) % cap
    south = adjoint_in[:, :, :cap, :].reshape(count, nlon)
    north = adjoint_in[:, :, nlat - cap:, :].reshape(count, nlon)
    south_cut = cutoffs[0].astype(jnp.float32)[row_cap]
    north_cut = cutoffs[1].astype(jnp.float32)[row_cap]
    south = filter_rows(south, south_cut).reshape(fields, levels, cap, nlon)
    north = filter_rows(north, north_cut).reshape(fields, levels, cap, nlon)
    filtered = jnp.concatenate([south, adjoint_in[:, :, cap:nlat - cap, :], north], 2)
    state = pad_field(trajectory)
    rows = jnp.arange(-1, nlat + 1, dtype=jnp.int32)

    def forward(delta):
        return out_region(pad_field(delta), state, rows, nlat)
    unused, pull = jax.vjp(forward, jnp.zeros_like(adjoint_in))
    return pull(filtered)[0]
```

```python
import functools

import jax
import jax.numpy as jnp
import ml_dtypes
import numpy as np
from jax import lax
from jax.experimental import pallas as pl
from jax.experimental.pallas import tpu as pltpu
from jax.sharding import PartitionSpec as P

MESH = pl.DeviceIdType.MESH
NLON, LEV, ROWS, LANES, LON, LAT = 2048, 32, 64, 128, 16, 8
PAIRS = 3 * LEV
HALF, CHUNKS = 32, 12
HOME, SINGLE, EACH = 5, 3, 2
SLOTS = 5
cx, cy, cg, ca = 0.25, 0.25, 0.3, 0.25


def tables():
    m = np.arange(LANES)[:, None]
    k = np.arange(LANES)[None, :]
    forward = np.zeros((8, 256, 256))
    inverse = np.zeros((8, 256, 256))
    wave = np.zeros((8, 256))

    def angle(freq):
        return 2.0 * np.pi / NLON * ((freq * m) % NLON)

    for q in range(1, 8):
        freq = 16 * k + q
        cos, sin = np.cos(angle(freq)), np.sin(angle(freq))
        forward[q] = np.block([[cos, -sin], [sin, cos]])
        inverse[q] = forward[q].T / NLON
        wave[q] = np.tile(np.minimum(freq, NLON - freq)[0], 2)
    index = np.arange(LANES)
    for at, q, is_cos, order in (
        (0, 0, index <= 64, np.where(index <= 64, index, index - 64)),
        (128, 8, index < 64, index % 64),
    ):
        freq = (16 * order + q)[None, :]
        block = np.where(is_cos[None, :], np.cos(angle(freq)), -np.sin(angle(freq)))
        weight = np.where((freq == 0) | (freq == NLON // 2), 1.0, 2.0)
        forward[0, at : at + 128, at : at + 128] = block
        inverse[0, at : at + 128, at : at + 128] = (block * weight).T / NLON
        wave[0, at : at + 128] = freq[0]
    both = np.stack([forward, inverse])
    high = both.astype(np.float32).astype(ml_dtypes.bfloat16)
    low = (both - high.astype(np.float64)).astype(np.float32).astype(ml_dtypes.bfloat16)
    damp = (1.0 / np.maximum(wave, 1.0) ** 2).astype(np.float32)
    return np.stack([high, low], 1), damp


def cadd(a, b, sign=1.0):
    re = a[0] + b[0] if sign > 0 else a[0] - b[0]
    if a[1] is None and b[1] is None:
        return (re, None)
    if a[1] is None:
        return (re, b[1] if sign > 0 else -b[1])
    if b[1] is None:
        return (re, a[1])
    return (re, a[1] + b[1] if sign > 0 else a[1] - b[1])


def conj(a):
    return a if a[1] is None else (a[0], -a[1])


def ctwist(a, k, n, sign):
    if k == 0:
        return a
    re, im = a
    if 4 * k == n:
        if im is None:
            return (jnp.zeros_like(re), re if sign > 0 else -re)
        return (-im, re) if sign > 0 else (im, -re)
    c, s = float(np.cos(2 * np.pi * k / n)), sign * float(np.sin(2 * np.pi * k / n))
    if im is None:
        return (re * c, re * s)
    if 8 * k == n:
        return ((re - im) * c, (re + im) * c) if sign > 0 else ((re + im) * c, (im - re) * c)
    return (re * c - im * s, re * s + im * c)


def real_dft(xs):
    n = len(xs)
    if n == 1:
        return [(xs[0], None)]
    if n == 2:
        return [(xs[0] + xs[1], None), (xs[0] - xs[1], None)]
    even, odd = real_dft(xs[0::2]), real_dft(xs[1::2])
    out = [None] * (n // 2 + 1)
    for k in range(n // 4 + 1):
        turned = ctwist(odd[k], k, n, -1)
        out[k] = cadd(even[k], turned)
        if k != n // 4:
            out[n // 2 - k] = conj(cadd(even[k], turned, -1.0))
    return out


def real_inverse(spec):
    n = 2 * (len(spec) - 1)
    if n == 2:
        return [spec[0][0] + spec[1][0], spec[0][0] - spec[1][0]]
    even, odd = [], []
    for k in range(n // 4 + 1):
        other = conj(spec[n // 2 - k])
        even.append(cadd(spec[k], other))
        odd.append(ctwist(cadd(spec[k], other, -1.0), k, n, 1))
    for part in (even, odd):
        part[0] = (part[0][0], None)
        part[-1] = (part[-1][0], None)
    a, b = real_inverse(even), real_inverse(odd)
    return [v for both in zip(a, b) for v in both]


def product(z, high, low):
    hi = z.astype(jnp.bfloat16)
    lo = (z - hi.astype(jnp.float32)).astype(jnp.bfloat16)
    rows = z.shape[0]
    main = jnp.dot(jnp.concatenate([hi, lo], 0), high, preferred_element_type=jnp.float32)
    rest = jnp.dot(hi, low, preferred_element_type=jnp.float32)
    return main[:rows] + main[rows:] + rest


def filter_chunk(blocks, table, damp_of):
    spec = real_dft(blocks)
    groups = [jnp.concatenate([spec[0][0], spec[8][0]], 1)]
    groups += [jnp.concatenate(spec[q], 1) for q in range(1, 8)]
    back = []
    for q in range(8):
        waves = product(groups[q], table[0, 0, q], table[0, 1, q]) * damp_of(q)
        back.append(product(waves, table[1, 0, q], table[1, 1, q]))
    spec = [(back[0][:, :LANES], None)]
    spec += [(back[q][:, :LANES], back[q][:, LANES:]) for q in range(1, 8)]
    spec += [(back[0][:, LANES:], None)]
    return real_inverse(spec)


def flip_bits(value, mask, width=4):
    out = 0
    for bit in range(width):
        own = (value // (1 << bit)) % 2
        out = out + (1 << bit) * ((1 - own) if (mask >> bit) & 1 else own)
    return out


def exchange_kernel(
    adj, traj, cuts, inverse_k2, table_in,
    mu_out, ewt_out, ewm_out, ns_out,
    mu, trj, rin, rcv, yout, rout, table, damp, ew_send, ew_recv, ns_send, ns_recv,
    rin_sem, relay_sem, fs_sem, rcv_sem, bs_sem, rout_sem, ro_sem, mu_sem,
    ews_sem, ewr_sem, nss_sem, nsr_sem, local_sem,
):
    lon = lax.axis_index("lon")
    lat = lax.axis_index("lat")
    mirror = flip_bits(lon, 8)
    is_cap = (lat == 0) | (lat == LAT - 1)
    is_single = (lat == 2) | (lat == 5)
    is_double = (lat == 1) | (lat == 6)
    steps = jnp.where(is_cap, HOME, jnp.where(is_single, SINGLE, jnp.where(is_double, 2 * EACH, 0)))
    lower = lat < LAT // 2

    def to(lon_at, lat_at):
        return {"lon": lon_at, "lat": lat_at}

    peers = [to(flip_bits(lon, k), lat) for k in range(1, 16)]
    peers += [to(lon, (lat + k) % LAT) for k in (1, 2, 6, 7)]
    peers += [to(mirror, flip_bits(lat, 1, 3))]
    barrier = pltpu.get_barrier_semaphore()
    for peer in peers:
        pl.semaphore_signal(barrier, inc=1, device_id=peer, device_id_type=MESH)

    table_copy = pltpu.make_async_copy(table_in, table, local_sem.at[0])
    traj_copy = pltpu.make_async_copy(traj, trj, local_sem.at[1])
    mu_copy = pltpu.make_async_copy(adj, mu, local_sem.at[2])
    traj_copy.start()
    table_copy.start()

    @pl.when(jnp.logical_not(is_cap))
    def _():
        mu_copy.start()

    pl.semaphore_wait(barrier, len(peers))

    def chunk_of(ref, chunk):
        pair = pl.multiple_of(16 * (chunk // 2), 16)
        row = pl.multiple_of(HALF * (chunk % 2), HALF)
        return ref.at[pl.ds(pair, 16), pl.ds(row, HALF)]

    def relay(chunk, device, slot):
        pltpu.make_async_remote_copy(
            src_ref=chunk_of(adj, chunk), dst_ref=rin.at[slot],
            send_sem=relay_sem.at[chunk], recv_sem=rin_sem.at[slot],
            device_id=device, device_id_type=MESH,
        ).start()

    def step_of(s):
        odd = s % 2
        near, far = jnp.where(lower, 0, LAT - 1), jnp.where(lower, LAT - 1, 0)
        cap = jnp.where(is_double & (odd == 1), far, near)
        chunk = jnp.where(
            is_cap, s, jnp.where(is_single, HOME + s, HOME + SINGLE + EACH * odd + s // 2)
        )
        flip = jnp.where(is_double & (odd == 0), 1, 0)
        return cap, chunk, flip

    def all_to_all(src_at, dst_at, send_sem, recv_sem):
        for k in range(1, 16):
            member = flip_bits(lon, k)
            pltpu.make_async_remote_copy(
                src_ref=src_at(member), dst_ref=dst_at, send_sem=send_sem, recv_sem=recv_sem,
                device_id=to(member, lat), device_id_type=MESH,
            ).start()
        pltpu.make_async_copy(src_at(lon), dst_at, recv_sem).start()

    def home_lon(member, flip):
        return jnp.where(flip == 1, (member + 8) % 16, member)

    def forward(s):
        unused_cap, unused_chunk, flip = step_of(s)
        pltpu.make_async_copy(rin.at[s], rin.at[s], rin_sem.at[s]).wait()
        all_to_all(
            lambda member: rin.at[s, member], rcv.at[s, home_lon(lon, flip)], fs_sem.at[s], rcv_sem.at[s]
        )

    def backward(s):
        unused_cap, unused_chunk, flip = step_of(s)
        all_to_all(
            lambda member: yout.at[s, home_lon(member, flip)], rout.at[s, lon], bs_sem.at[s], rout_sem.at[s]
        )

    def work(s):
        cap, chunk, unused_flip = step_of(s)
        side = jnp.where(cap == 0, 0, 1)
        row = pl.multiple_of(HALF * (chunk % 2), HALF)
        pltpu.make_async_copy(rcv.at[s], rcv.at[s], rcv_sem.at[s]).wait()
        done = filter_chunk(
            [rcv[s, d] for d in range(16)], table, lambda q: damp[side, q, pl.ds(row, HALF), :]
        )
        for d in range(16):
            yout[s, d] = done[d]

    def deliver(s):
        cap, chunk, flip = step_of(s)
        pltpu.make_async_copy(rout.at[s], rout.at[s], rout_sem.at[s]).wait()

        @pl.when(is_cap)
        def _():
            pltpu.make_async_copy(rout.at[s], chunk_of(mu, chunk), mu_sem.at[chunk]).start()

        @pl.when(jnp.logical_not(is_cap))
        def _():
            pltpu.make_async_remote_copy(
                src_ref=rout.at[s], dst_ref=chunk_of(mu, chunk),
                send_sem=ro_sem.at[s], recv_sem=mu_sem.at[chunk],
                device_id=to(home_lon(lon, flip), cap), device_id_type=MESH,
            ).start()

    @pl.when(is_cap)
    def _():
        turn = jnp.where(lower, 2, LAT - 2)
        single, other = (lat + turn) % LAT, (lat + LAT - turn) % LAT
        for s in range(HOME):
            pltpu.make_async_copy(chunk_of(adj, s), rin.at[s], rin_sem.at[s]).start()
        for s in range(SINGLE):
            relay(HOME + s, to(lon, single), s)
            if s < EACH:
                relay(HOME + SINGLE + s, to(mirror, flip_bits(lat, 1, 3)), 2 * s)
                relay(HOME + SINGLE + EACH + s, to(lon, other), 2 * s + 1)

        @pl.loop(0, HOME)
        def _(s):
            forward(s)

    lane = lax.broadcasted_iota(jnp.int32, (ROWS, LANES), 1)

    def pack(ref, kind, other_field):
        def body(level, packed):
            west, east = packed
            for at, f in ((0, 0), (LEV, other_field)):
                target = at + level
                turned = pltpu.roll(ref[f * LEV + level], target, axis=1)
                west = jnp.where(lane == target, turned, west)
                east = jnp.where(lane == (target + LANES - 1) % LANES, turned, east)
            return west, east

        zero = jnp.zeros((ROWS, LANES), jnp.float32)
        west, east = lax.fori_loop(0, LEV, body, (zero, zero))
        ew_send[kind, 0] = west
        ew_send[kind, 1] = east

    def pack_rows(ref, kind):
        for at, f in ((0, 0), (LEV, 2)):
            @pl.loop(0, LEV)
            def _(level):
                ns_send[kind, 0, pl.ds(at + level, 1), :] = ref[f * LEV + level, 0:1, :]
                ns_send[kind, 1, pl.ds(at + level, 1), :] = ref[f * LEV + level, ROWS - 1 : ROWS, :]

    def halo_copies(kind):
        ew, ns = [], []
        for side, step in ((0, LON - 1), (1, 1)):
            ew.append(pltpu.make_async_remote_copy(
                src_ref=ew_send.at[kind, side], dst_ref=ew_recv.at[kind, 1 - side],
                send_sem=ews_sem.at[kind, side], recv_sem=ewr_sem.at[kind, 1 - side],
                device_id=to((lon + step) % LON, lat), device_id_type=MESH,
            ))
        for side, step in ((0, LAT - 1), (1, 1)):
            ns.append(pltpu.make_async_remote_copy(
                src_ref=ns_send.at[kind, side], dst_ref=ns_recv.at[kind, 1 - side],
                send_sem=nss_sem.at[kind, side], recv_sem=nsr_sem.at[kind, 1 - side],
                device_id=to(lon, (lat + step) % LAT), device_id_type=MESH,
            ))
        return ew, ns

    def send_halos(ref, kind, ew_field):
        pack(ref, kind, ew_field)
        pack_rows(ref, kind)
        ew, ns = halo_copies(kind)
        ew[0].start()
        ew[1].start()

        @pl.when(lat > 0)
        def _():
            ns[0].start()

        @pl.when(lat < LAT - 1)
        def _():
            ns[1].start()

    traj_copy.wait()
    send_halos(trj, 0, 1)

    @pl.when(jnp.logical_not(is_cap))
    def _():
        mu_copy.wait()
        send_halos(mu, 1, 1)

    row_at = lax.broadcasted_iota(jnp.int32, (ROWS, ROWS), 0)
    col_at = lax.broadcasted_iota(jnp.int32, (ROWS, ROWS), 1)
    for side in range(2):
        cut = cuts[side : side + 1, :].astype(jnp.float32)
        column = jnp.sum(jnp.where(row_at == col_at, cut, 0.0), axis=1, keepdims=True)
        for q in range(8):
            damp[side, q] = jnp.minimum(1.0, column * column * inverse_k2[q : q + 1, :])
    table_copy.wait()

    @pl.loop(0, steps + 2)
    def _(t):
        @pl.when(jnp.logical_not(is_cap) & (t < steps))
        def _():
            forward(t)

        @pl.when((t >= 1) & (t <= steps))
        def _():
            work(t - 1)
            backward(t - 1)

        @pl.when((t >= 2) & (steps > 0))
        def _():
            deliver(t - 2)

    @pl.when(is_cap)
    def _():
        for chunk in range(CHUNKS):
            part = chunk_of(mu, chunk)
            pltpu.make_async_copy(part, part, mu_sem.at[chunk]).wait()
        send_halos(mu, 1, 1)

    out_copy = pltpu.make_async_copy(mu, mu_out, local_sem.at[3])
    out_copy.start()

    @pl.when(is_cap)
    def _():
        for chunk in range(HOME, CHUNKS):
            part = chunk_of(mu, chunk)
            pltpu.make_async_copy(part, part, relay_sem.at[chunk]).wait()

    @pl.loop(0, steps)
    def _(s):
        most = rin.at[s, pl.ds(0, 15)]
        pltpu.make_async_copy(most, most, fs_sem.at[s]).wait()
        pltpu.make_async_copy(most, most, bs_sem.at[s]).wait()

        @pl.when(jnp.logical_not(is_cap))
        def _():
            pltpu.make_async_copy(rin.at[s], rin.at[s], ro_sem.at[s]).wait()

    for kind in range(2):
        ew, ns = halo_copies(kind)
        ew[0].wait()
        ew[1].wait()
        for side, here in ((0, lat > 0), (1, lat < LAT - 1)):
            @pl.when(here)
            def _():
                ns[side].wait_send()
                whole = ns_recv.at[kind, side]
                pltpu.make_async_copy(whole, whole, nsr_sem.at[kind, side]).wait()
                ns_out[kind, side] = ns_recv[kind, side]

            @pl.when(jnp.logical_not(here))
            def _():
                ns_out[kind, side] = jnp.zeros((2 * LEV, LANES), jnp.float32)

    ewt_out[...] = ew_recv[0]
    ewm_out[...] = ew_recv[1]
    out_copy.wait()


LEVELS_STEP = 4


def stencil_kernel(traj, mu, ewt, ewm, ns, out):
    lat = lax.axis_index("lat")
    first = pl.program_id(0) * LEVELS_STEP
    row = lax.broadcasted_iota(jnp.int32, (ROWS, LANES), 0)
    lane = lax.broadcasted_iota(jnp.int32, (ROWS, LANES), 1)
    no_south = (row == 0) & (lat == 0)
    no_north = (row == ROWS - 1) & (lat == LAT - 1)

    def level_step(j, unused):
        level = first + j

        def east_west(x, halo, at):
            from_west = jnp.where(lane == LANES - 1, pltpu.roll(halo[0], (2 * LANES - at) % LANES, axis=1), x)
            from_east = jnp.where(lane == 0, pltpu.roll(halo[1], (2 * LANES - at) % LANES, axis=1), x)
            return pltpu.roll(from_west, 1, axis=1), pltpu.roll(from_east, LANES - 1, axis=1)

        def south_north(x, kind, at):
            south = jnp.broadcast_to(ns[kind, 0, pl.ds(at + level, 1), :], (ROWS, LANES))
            north = jnp.broadcast_to(ns[kind, 1, pl.ds(at + level, 1), :], (ROWS, LANES))
            return (
                jnp.where(row == 0, south, pltpu.roll(x, 1, axis=0)),
                jnp.where(row == ROWS - 1, north, pltpu.roll(x, ROWS - 1, axis=0)),
            )

        H, U, V = (traj[f, j] for f in range(3))
        p, q, r = (mu[f, j] for f in range(3))
        H_w, H_e = east_west(H, ewt, level)
        U_w, U_e = east_west(U, ewt, LEV + level)
        p_w, p_e = east_west(p, ewm, level)
        q_w, q_e = east_west(q, ewm, LEV + level)
        H_s, H_n = south_north(H, 0, 0)
        V_s, V_n = south_north(V, 0, LEV)
        p_s, p_n = south_north(p, 1, 0)
        r_s, r_n = south_north(r, 1, LEV)
        gx_e, gx_w = (0.25 * cx) * (p_e - p), (0.25 * cx) * (p - p_w)
        gy_n = jnp.where(no_north, 0.0, (0.25 * cy) * (p_n - p))
        gy_s = jnp.where(no_south, 0.0, (0.25 * cy) * (p - p_s))
        out[0, j] = (
            p + ((U + U_e) * gx_e + (U_w + U) * gx_w) + ((V + V_n) * gy_n + (V_s + V) * gy_s)
            + cg * ((q_e - q_w) + (r_n - r_s))
        )
        out[1, j] = q + ca * (U_e * q_e - U_w * q_w) + ((H + H_e) * gx_e + (H_w + H) * gx_w)
        out[2, j] = r + ca * (V_n * r_n - V_s * r_s) + ((H + H_n) * gy_n + (H_s + H) * gy_s)
        return unused

    lax.fori_loop(0, LEVELS_STEP, level_step, 0)


TABLES, INVERSE_K2 = tables()


def per_device(trajectory, adjoint_in, cutoffs):
    f32 = jnp.float32
    whole = pl.BlockSpec(memory_space=pltpu.VMEM)
    anywhere = pl.BlockSpec(memory_space=pl.ANY)
    slots = pltpu.VMEM((SLOTS, 16, HALF, LANES), f32)
    dma = pltpu.SemaphoreType.DMA
    mu, ewt, ewm, ns = pl.pallas_call(
        exchange_kernel,
        out_shape=(
            jax.ShapeDtypeStruct((PAIRS, ROWS, LANES), f32),
            jax.ShapeDtypeStruct((2, ROWS, LANES), f32),
            jax.ShapeDtypeStruct((2, ROWS, LANES), f32),
            jax.ShapeDtypeStruct((2, 2, 2 * LEV, LANES), f32),
        ),
        in_specs=[anywhere, anywhere, whole, whole, anywhere],
        out_specs=(anywhere, whole, whole, whole),
        scratch_shapes=[
            pltpu.VMEM((PAIRS, ROWS, LANES), f32),
            pltpu.VMEM((PAIRS, ROWS, LANES), f32),
            slots, slots, slots, slots,
            pltpu.VMEM((2, 2, 8, 256, 256), jnp.bfloat16),
            pltpu.VMEM((2, 8, ROWS, 256), f32),
            pltpu.VMEM((2, 2, ROWS, LANES), f32),
            pltpu.VMEM((2, 2, ROWS, LANES), f32),
            pltpu.VMEM((2, 2, 2 * LEV, LANES), f32),
            pltpu.VMEM((2, 2, 2 * LEV, LANES), f32),
            dma((SLOTS,)), dma((CHUNKS,)), dma((SLOTS,)), dma((SLOTS,)), dma((SLOTS,)), dma((SLOTS,)),
            dma((SLOTS,)), dma((CHUNKS,)),
            dma((2, 2)), dma((2, 2)), dma((2, 2)), dma((2, 2)), dma((4,)),
        ],
        compiler_params=pltpu.CompilerParams(
            collective_id=0, has_side_effects=True, vmem_limit_bytes=48 << 20
        ),
        name="exchange_filter",
    )(
        adjoint_in.reshape(PAIRS, ROWS, LANES),
        trajectory.reshape(PAIRS, ROWS, LANES),
        cutoffs,
        jnp.asarray(INVERSE_K2),
        jnp.asarray(TABLES),
    )
    field = pl.BlockSpec((3, LEVELS_STEP, ROWS, LANES), lambda i: (0, i, 0, 0))
    return pl.pallas_call(
        stencil_kernel,
        grid=(LEV // LEVELS_STEP,),
        out_shape=jax.ShapeDtypeStruct((3, LEV, ROWS, LANES), f32),
        in_specs=[field, field, whole, whole, whole],
        out_specs=field,
        compiler_params=pltpu.CompilerParams(vmem_limit_bytes=24 << 20),
        name="adjoint_stencil",
    )(trajectory, mu.reshape(3, LEV, ROWS, LANES), ewt, ewm, ns)


def solution(mesh):
    in_specs = (P(None, None, "lat", "lon"), P(None, None, "lat", "lon"), P())
    out_specs = P(None, None, "lat", "lon")
    return jax.shard_map(
        per_device, mesh=mesh, in_specs=in_specs, out_specs=out_specs, check_vma=False
    )
```

```python
import functools

import jax
import jax.numpy as jnp
import ml_dtypes
import numpy as np
from jax import lax
from jax.experimental import pallas as pl
from jax.experimental.pallas import tpu as pltpu
from jax.sharding import PartitionSpec as P

MESH = pl.DeviceIdType.MESH
NLON, LEV, ROWS, LANES, LON, LAT = 2048, 32, 64, 128, 16, 8
PAIRS = 3 * LEV
GROUP, HALF, CHUNKS = 8, 32, 24
HOME, SINGLE, NEAR, FAR = (7, 4), (3, 2), (3, 1), (3, 1)
LAG = 2
SLOTS = max(sum(HOME), sum(SINGLE), 2 * sum(NEAR))
cx, cy, cg, ca = 0.25, 0.25, 0.3, 0.25


def tables():
    m = np.arange(LANES)[:, None]
    k = np.arange(LANES)[None, :]
    forward = np.zeros((8, 256, 256))
    inverse = np.zeros((8, 256, 256))
    wave = np.zeros((8, 256))

    def angle(freq):
        return 2.0 * np.pi / NLON * ((freq * m) % NLON)

    for q in range(1, 8):
        freq = 16 * k + q
        cos, sin = np.cos(angle(freq)), np.sin(angle(freq))
        forward[q] = np.block([[cos, -sin], [sin, cos]])
        inverse[q] = forward[q].T / NLON
        wave[q] = np.tile(np.minimum(freq, NLON - freq)[0], 2)
    index = np.arange(LANES)
    for at, q, is_cos, order in (
        (0, 0, index <= 64, np.where(index <= 64, index, index - 64)),
        (128, 8, index < 64, index % 64),
    ):
        freq = (16 * order + q)[None, :]
        block = np.where(is_cos[None, :], np.cos(angle(freq)), -np.sin(angle(freq)))
        weight = np.where((freq == 0) | (freq == NLON // 2), 1.0, 2.0)
        forward[0, at : at + 128, at : at + 128] = block
        inverse[0, at : at + 128, at : at + 128] = (block * weight).T / NLON
        wave[0, at : at + 128] = freq[0]
    both = np.stack([forward, inverse])
    high = both.astype(np.float32).astype(ml_dtypes.bfloat16)
    low = (both - high.astype(np.float64)).astype(np.float32).astype(ml_dtypes.bfloat16)
    damp = (1.0 / np.maximum(wave, 1.0) ** 2).astype(np.float32)
    return np.stack([high, low], 1), damp


def cadd(a, b, sign=1.0):
    re = a[0] + b[0] if sign > 0 else a[0] - b[0]
    if a[1] is None and b[1] is None:
        return (re, None)
    if a[1] is None:
        return (re, b[1] if sign > 0 else -b[1])
    if b[1] is None:
        return (re, a[1])
    return (re, a[1] + b[1] if sign > 0 else a[1] - b[1])


def conj(a):
    return a if a[1] is None else (a[0], -a[1])


def ctwist(a, k, n, sign):
    if k == 0:
        return a
    re, im = a
    if 4 * k == n:
        if im is None:
            return (jnp.zeros_like(re), re if sign > 0 else -re)
        return (-im, re) if sign > 0 else (im, -re)
    c, s = float(np.cos(2 * np.pi * k / n)), sign * float(np.sin(2 * np.pi * k / n))
    if im is None:
        return (re * c, re * s)
    if 8 * k == n:
        return ((re - im) * c, (re + im) * c) if sign > 0 else ((re + im) * c, (im - re) * c)
    return (re * c - im * s, re * s + im * c)


def real_dft(xs):
    n = len(xs)
    if n == 1:
        return [(xs[0], None)]
    if n == 2:
        return [(xs[0] + xs[1], None), (xs[0] - xs[1], None)]
    even, odd = real_dft(xs[0::2]), real_dft(xs[1::2])
    out = [None] * (n // 2 + 1)
    for k in range(n // 4 + 1):
        turned = ctwist(odd[k], k, n, -1)
        out[k] = cadd(even[k], turned)
        if k != n // 4:
            out[n // 2 - k] = conj(cadd(even[k], turned, -1.0))
    return out


def real_inverse(spec):
    n = 2 * (len(spec) - 1)
    if n == 2:
        return [spec[0][0] + spec[1][0], spec[0][0] - spec[1][0]]
    even, odd = [], []
    for k in range(n // 4 + 1):
        other = conj(spec[n // 2 - k])
        even.append(cadd(spec[k], other))
        odd.append(ctwist(cadd(spec[k], other, -1.0), k, n, 1))
    for part in (even, odd):
        part[0] = (part[0][0], None)
        part[-1] = (part[-1][0], None)
    a, b = real_inverse(even), real_inverse(odd)
    return [v for both in zip(a, b) for v in both]


def product(z, high, low):
    hi = z.astype(jnp.bfloat16)
    lo = (z - hi.astype(jnp.float32)).astype(jnp.bfloat16)
    rows = z.shape[0]
    main = jnp.dot(jnp.concatenate([hi, lo], 0), high, preferred_element_type=jnp.float32)
    rest = jnp.dot(hi, low, preferred_element_type=jnp.float32)
    return main[:rows] + main[rows:] + rest


def filter_chunk(blocks, table, damp_of):
    spec = real_dft(blocks)
    groups = [jnp.concatenate([spec[0][0], spec[8][0]], 1)]
    groups += [jnp.concatenate(spec[q], 1) for q in range(1, 8)]
    back = []
    for q in range(8):
        waves = product(groups[q], table[0, 0, q], table[0, 1, q]) * damp_of(q)
        back.append(product(waves, table[1, 0, q], table[1, 1, q]))
    spec = [(back[0][:, :LANES], None)]
    spec += [(back[q][:, :LANES], back[q][:, LANES:]) for q in range(1, 8)]
    spec += [(back[0][:, LANES:], None)]
    return real_inverse(spec)


def flip_bits(value, mask, width=4):
    out = 0
    for bit in range(width):
        own = (value // (1 << bit)) % 2
        out = out + (1 << bit) * ((1 - own) if (mask >> bit) & 1 else own)
    return out


def numbered(kind, index, side):
    kinds = (HOME, SINGLE, NEAR, FAR)
    early, late = kinds[kind]
    first = sum(k[0] for k in kinds[:kind])
    beside = sum(k[1] - 1 for k in kinds[:kind])
    base = 2 * CHUNKS // 3
    last = base + 2 * kind + side
    before = base + 2 * (beside + index - early) + 1 - side
    return jnp.where(index < early, first + index, jnp.where(index == early + late - 1, last, before))


def exchange_kernel(
    adj, traj, cuts_in, inverse_k2_in, table_in,
    mu_out, ew_out, ns_out,
    mu, trj, rin, rcv, yout, table, damp, cuts, inverse_k2, ew_send, ew_recv, ns_send, ns_recv,
    rin_sem, relay_sem, fs_sem, rcv_sem, bs_sem, ro_sem, mu_sem,
    ews_sem, ewr_sem, nss_sem, nsr_sem, local_sem,
):
    lon = lax.axis_index("lon")
    lat = lax.axis_index("lat")
    core, chip = lon % 2, lon // 2
    mirror = flip_bits(lon, 8)
    own_side = jnp.where(lat < LAT // 2, 0, 1)
    is_cap = (lat == 0) | (lat == LAT - 1)
    is_single = (lat == 2) | (lat == 5)
    is_double = (lat == 1) | (lat == 6)
    helps = is_single | is_double
    lower = lat < LAT // 2
    waves = jnp.where(is_cap, sum(HOME), jnp.where(is_single, sum(SINGLE), jnp.where(is_double, sum(NEAR), 0)))
    width = jnp.where(is_double, 2, 1)
    lead, lag = jnp.where(is_cap, 0, 1), jnp.where(is_cap, 0, LAG)

    def to(lon_at, lat_at):
        return {"lon": lon_at, "lat": lat_at}

    peers = [to(flip_bits(lon, k), lat) for k in range(1, 16)]
    peers += [to(lon, (lat + k) % LAT) for k in (1, 2, 6, 7)]
    peers += [to(mirror, flip_bits(lat, 1, 3))]
    barrier = pltpu.get_barrier_semaphore()
    for peer in peers:
        pl.semaphore_signal(barrier, inc=1, device_id=peer, device_id_type=MESH)

    traj_copy = pltpu.make_async_copy(traj, trj, local_sem.at[1])
    mu_copy = pltpu.make_async_copy(adj, mu.at[pl.ds(0, PAIRS)], local_sem.at[2])
    small_copies = [
        pltpu.make_async_copy(cuts_in, cuts, local_sem.at[3]),
        pltpu.make_async_copy(inverse_k2_in, inverse_k2, local_sem.at[4]),
        pltpu.make_async_copy(table_in, table, local_sem.at[0]),
    ]

    def chunk_of(ref, chunk):
        pair = pl.multiple_of(GROUP * (chunk // 2), GROUP)
        row = pl.multiple_of(HALF * (chunk % 2), HALF)
        return ref.at[pl.ds(pair, GROUP), pl.ds(row, HALF)]

    @pl.when(is_cap)
    def _():
        for s in range(sum(HOME)):
            pltpu.make_async_copy(chunk_of(adj, numbered(0, s, own_side)), rin.at[s], rin_sem.at[s]).start()

    traj_copy.start()
    for copy in small_copies:
        copy.start()

    @pl.when(jnp.logical_not(is_cap))
    def _():
        mu_copy.start()

    pl.semaphore_wait(barrier, len(peers))

    def relay(chunk, device, slot):
        pltpu.make_async_remote_copy(
            src_ref=chunk_of(adj, chunk), dst_ref=rin.at[slot],
            send_sem=relay_sem.at[chunk], recv_sem=rin_sem.at[slot],
            device_id=device, device_id_type=MESH,
        ).start()

    def step_of(s):
        odd = s % 2
        far = is_double & (odd == 1)
        side = jnp.where(far, 1 - own_side, own_side)
        double = jnp.where(odd == 1, numbered(3, s // 2, side), numbered(2, s // 2, side))
        chunk = jnp.where(is_cap, numbered(0, s, side), jnp.where(is_single, numbered(1, s, side), double))
        flip = jnp.where(is_double & (odd == 0), 1, 0)
        return side, chunk, flip

    def home_lon(member, flip):
        return jnp.where(flip == 1, (member + 8) % 16, member)

    def landing(s):
        unused_side, chunk, unused_flip = step_of(s)
        return jnp.where(is_cap, chunk, 2 * PAIRS // GROUP + s)

    def remote(src, dst, send_sem, recv_sem, member):
        pltpu.make_async_remote_copy(
            src_ref=src, dst_ref=dst, send_sem=send_sem, recv_sem=recv_sem,
            device_id=to(member, lat), device_id_type=MESH,
        ).start()

    def forward(s):
        unused_side, unused_chunk, flip = step_of(s)
        pltpu.make_async_copy(rin.at[s], rin.at[s], rin_sem.at[s]).wait()
        dst = rcv.at[s, home_lon(lon, flip)]
        for k in range(1, 8):
            owner = flip_bits(chip, k, 3)
            remote(rin.at[s, owner], dst, fs_sem.at[s], rcv_sem.at[s], 2 * owner + s % 2)

        @pl.when(core == s % 2)
        def _():
            pltpu.make_async_copy(rin.at[s, chip], dst, rcv_sem.at[s]).start()

        @pl.when(core != s % 2)
        def _():
            remote(rin.at[s, chip], dst, fs_sem.at[s], rcv_sem.at[s], 2 * chip + 1 - core)

    def work(s):
        side, chunk, flip = step_of(s)
        row = pl.multiple_of(HALF * (chunk % 2), HALF)
        pltpu.make_async_copy(rcv.at[s], rcv.at[s], rcv_sem.at[s]).wait()
        done = filter_chunk(
            [rcv[s, d] for d in range(16)], table, lambda q: damp[side, q, pl.ds(row, HALF), :]
        )
        for d in range(16):
            yout[s, d] = done[d]
        land = landing(s)
        pair = GROUP * (land // 2) + chip
        dst = mu.at[pair, pl.ds(pl.multiple_of(HALF * (land % 2), HALF), HALF)]
        for k in range(1, 16):
            member = flip_bits(lon, k)
            remote(yout.at[s, home_lon(member, flip)], dst, bs_sem.at[s], mu_sem.at[land], member)
        pltpu.make_async_copy(yout.at[s, home_lon(lon, flip)], dst, mu_sem.at[land]).start()

    def deliver(s):
        side, chunk, flip = step_of(s)
        part = chunk_of(mu, landing(s))
        pltpu.make_async_copy(part, part, mu_sem.at[landing(s)]).wait()
        pltpu.make_async_remote_copy(
            src_ref=part, dst_ref=chunk_of(mu, chunk), send_sem=ro_sem.at[s], recv_sem=mu_sem.at[chunk],
            device_id=to(home_lon(lon, flip), (LAT - 1) * side), device_id_type=MESH,
        ).start()

    @pl.when(is_cap)
    def _():
        turn = jnp.where(lower, 2, LAT - 2)
        single, other = (lat + turn) % LAT, (lat + LAT - turn) % LAT
        outer = to(mirror, flip_bits(lat, 1, 3))
        for s in range(max(sum(SINGLE), sum(NEAR))):
            if s < sum(NEAR):
                relay(numbered(2, s, own_side), outer, 2 * s)
                relay(numbered(3, s, own_side), to(lon, other), 2 * s + 1)
            if s < sum(SINGLE):
                relay(numbered(1, s, own_side), to(lon, single), s)

        @pl.loop(0, sum(HOME))
        def _(s):
            forward(s)

    lane = lax.broadcasted_iota(jnp.int32, (ROWS, LANES), 1)

    def pack(ref, kind):
        def body(level, packed):
            for at, f in ((0, 0), (LANES // 2, 1)):
                target = at + 2 * level
                turned = pltpu.roll(ref[f * LEV + level], target, axis=1)
                packed = jnp.where((lane == target) | (lane == (target + LANES - 1) % LANES), turned, packed)
            return packed

        ew_send[kind] = lax.fori_loop(0, LEV, body, jnp.zeros((ROWS, LANES), jnp.float32))

    def pack_rows(ref, kind, side):
        at = (0, ROWS - 1)[side]
        for first, f in ((0, 0), (LEV, 2)):
            @pl.loop(0, LEV)
            def _(level):
                ns_send[kind, side, pl.ds(first + level, 1), :] = ref[f * LEV + level, at : at + 1, :]

    def ew_copies(kind):
        return [
            pltpu.make_async_remote_copy(
                src_ref=ew_send.at[kind], dst_ref=ew_recv.at[kind, 1 - side],
                send_sem=ews_sem.at[kind, side], recv_sem=ewr_sem.at[kind, 1 - side],
                device_id=to((lon + step) % LON, lat), device_id_type=MESH,
            )
            for side, step in ((0, LON - 1), (1, 1))
        ]

    def ns_copies(kind):
        return [
            pltpu.make_async_remote_copy(
                src_ref=ns_send.at[kind, side], dst_ref=ns_recv.at[kind, 1 - side],
                send_sem=nss_sem.at[kind, side], recv_sem=nsr_sem.at[kind, 1 - side],
                device_id=to(lon, (lat + step) % LAT), device_id_type=MESH,
            )
            for side, step in ((0, LAT - 1), (1, 1))
        ]

    inner = (lat > 0, lat < LAT - 1)

    def send_columns(ref, kind):
        pack(ref, kind)
        for copy in ew_copies(kind):
            copy.start()

    def send_rows(ref, kind):
        for side, copy in enumerate(ns_copies(kind)):
            @pl.when(inner[side])
            def _():
                pack_rows(ref, kind, side)
                copy.start()

    traj_copy.wait()
    send_columns(trj, 0)
    send_rows(trj, 0)

    @pl.when(jnp.logical_not(is_cap))
    def _():
        mu_copy.wait()
        send_columns(mu, 1)
        send_rows(mu, 1)

    row_at = lax.broadcasted_iota(jnp.int32, (ROWS, ROWS), 0)
    col_at = lax.broadcasted_iota(jnp.int32, (ROWS, ROWS), 1)
    for copy in small_copies:
        copy.wait()
    for side in range(2):
        cut = cuts[side : side + 1, :].astype(jnp.float32)
        column = jnp.sum(jnp.where(row_at == col_at, cut, 0.0), axis=1, keepdims=True)
        for q in range(8):
            damp[side, q] = jnp.minimum(1.0, column * column * inverse_k2[q : q + 1, :])

    @pl.loop(0, jnp.where(waves > 0, waves + lag, 0))
    def _(t):
        for j in range(2):
            @pl.when(helps & (t < waves) & (j < width))
            def _():
                forward(t * width + j)

        s = jnp.where(is_double, (t - lead) * 2 + core, t - lead)

        @pl.when((t >= lead) & (t < waves + lead) & (s % 2 == core))
        def _():
            work(s)

        for j in range(2):
            @pl.when(helps & (t >= lag) & (j < width))
            def _():
                deliver((t - lag) * width + j)

    def arrived(chunk):
        part = chunk_of(mu, chunk)
        pltpu.make_async_copy(part, part, mu_sem.at[chunk]).wait()

    def out_copy(first, count, sem):
        return pltpu.make_async_copy(
            mu.at[pl.ds(first, count)], mu_out.at[pl.ds(first, count)], local_sem.at[sem]
        )

    early = 2 * CHUNKS // 3

    @pl.when(is_cap)
    def _():
        for chunk in range(early):
            arrived(chunk)
        send_columns(mu, 1)
        for group in range(CHUNKS // 6):
            arrived(early + 2 * group + 1 - own_side)
        send_rows(mu, 1)

    out_copy(0, 2 * LEV, 5).start()

    for kind in range(2):
        for copy in ew_copies(kind):
            copy.wait()
    even = lane % 2 == 0
    first_part = (lane < LANES // 2 - 1) | (lane == LANES - 1)

    def swapped(x):
        return pltpu.roll(x, LANES // 2, axis=1)

    def beyond(kind):
        return jnp.where(
            even, pltpu.roll(ew_recv[kind, 0], 1, axis=1), pltpu.roll(ew_recv[kind, 1], LANES - 1, axis=1)
        )

    state, state_out = ew_send[0], beyond(0)
    adjoint, adjoint_out = ew_send[1], beyond(1)
    p_in = jnp.where(first_part, adjoint, swapped(adjoint))
    p_out = jnp.where(first_part, adjoint_out, swapped(adjoint_out))
    q_out = jnp.where(first_part, swapped(adjoint_out), adjoint_out)
    term = (0.25 * cx) * (swapped(state) + swapped(state_out)) * (p_out - p_in)
    term = term + jnp.where(first_part, cg, ca * state_out) * q_out
    ew_out[...] = jnp.where(even, -term, term)

    for side in range(2):
        @pl.when(inner[side])
        def _():
            for kind in range(2):
                ns_copies(kind)[side].wait_send()
                whole = ns_recv.at[kind, side]
                pltpu.make_async_copy(whole, whole, nsr_sem.at[kind, side]).wait()
            H_in, V_in = ns_send[0, side, :LEV], ns_send[0, side, LEV:]
            H_out, V_out = ns_recv[0, side, :LEV], ns_recv[0, side, LEV:]
            p_diff = (0.25 * cy) * (ns_recv[1, side, :LEV] - ns_send[1, side, :LEV])
            r_out = ns_recv[1, side, LEV:]
            sign = 1.0 if side else -1.0
            ns_out[side, :LEV] = sign * ((V_in + V_out) * p_diff + cg * r_out)
            ns_out[side, LEV:] = sign * ((H_in + H_out) * p_diff + ca * V_out * r_out)

        @pl.when(jnp.logical_not(inner[side]))
        def _():
            ns_out[side] = jnp.zeros((2 * LEV, LANES), jnp.float32)

    @pl.when(is_cap)
    def _():
        for group in range(CHUNKS // 6):
            arrived(early + 2 * group + own_side)

    out_copy(2 * LEV, LEV, 6).start()

    @pl.when(is_cap)
    def _():
        for kind in (1, 2, 3):
            for s in range(sum((HOME, SINGLE, NEAR, FAR)[kind])):
                chunk = numbered(kind, s, own_side)
                part = chunk_of(mu, chunk)
                pltpu.make_async_copy(part, part, relay_sem.at[chunk]).wait()

    @pl.loop(0, waves * width)
    def _(s):
        most = rin.at[s, pl.ds(0, 7)]

        @pl.when(core == s % 2)
        def _():
            pltpu.make_async_copy(most, most, fs_sem.at[s]).wait()
            sent = rcv.at[s, pl.ds(0, 15)]
            pltpu.make_async_copy(sent, sent, bs_sem.at[s]).wait()

        @pl.when(core != s % 2)
        def _():
            pltpu.make_async_copy(rin.at[s], rin.at[s], fs_sem.at[s]).wait()

        @pl.when(helps)
        def _():
            pltpu.make_async_copy(rin.at[s], rin.at[s], ro_sem.at[s]).wait()

    out_copy(0, 2 * LEV, 5).wait()
    out_copy(2 * LEV, LEV, 6).wait()


LEVELS_STEP = 8


def stencil_kernel(traj, mu, ew, ns, out):
    first = pl.program_id(0) * LEVELS_STEP
    row = lax.broadcasted_iota(jnp.int32, (ROWS, LANES), 0)
    lane = lax.broadcasted_iota(jnp.int32, (ROWS, LANES), 1)
    edge = (lane == 0) | (lane == LANES - 1)

    def fluxes(p, a, b, r, axis):
        size = (ROWS, LANES)[axis]
        last = (row, lane)[axis] == size - 1

        def after(x):
            return pltpu.roll(x, size - 1, axis=axis)

        a_after = after(a)
        slope = jnp.where(last, 0.0, (0.25 * cx) * (after(p) - p))
        r_after = jnp.where(last, 0.0, after(r))
        r_here = jnp.where(last, 0.0, r)
        flux_h = (a + a_after) * slope
        flux_r = (b + after(b)) * slope
        to_h = (flux_h + cg * r_after) + pltpu.roll(flux_h - cg * r_here, 1, axis=axis)
        to_r = (flux_r + ca * (a_after * r_after)) + pltpu.roll(flux_r - ca * (a * r_here), 1, axis=axis)
        return to_h, to_r

    for j in range(LEVELS_STEP):
        level = first + j
        H, U, V = (traj[f, j] for f in range(3))
        p, q, r = (mu[f, j] for f in range(3))
        x_h, x_u = fluxes(p, U, H, q, 1)
        y_h, y_v = fluxes(p, V, H, r, 0)
        over_h = jnp.where(edge, pltpu.roll(ew[...], (LANES - 2 * level) % LANES, axis=1), 0.0)
        over_u = jnp.where(edge, pltpu.roll(ew[...], (LANES + LANES // 2 - 2 * level) % LANES, axis=1), 0.0)
        out[0, j] = p + x_h + y_h + over_h
        out[1, j] = q + x_u + over_u
        out[2, j] = r + y_v
        for side, at in ((0, 0), (1, ROWS - 1)):
            out[0, j, at : at + 1, :] += ns[side, pl.ds(level, 1), :]
            out[2, j, at : at + 1, :] += ns[side, pl.ds(LEV + level, 1), :]


TABLES, INVERSE_K2 = tables()


def per_device(trajectory, adjoint_in, cutoffs):
    f32 = jnp.float32
    whole = pl.BlockSpec(memory_space=pltpu.VMEM)
    anywhere = pl.BlockSpec(memory_space=pl.ANY)
    vmem = pltpu.VMEM
    dma = pltpu.SemaphoreType.DMA
    extra = GROUP * ((2 * sum(NEAR) + 1) // 2)
    if sum(SINGLE) > 2 * sum(NEAR):
        extra = GROUP * ((sum(SINGLE) + 1) // 2)
    mu, ew, ns = pl.pallas_call(
        exchange_kernel,
        out_shape=(
            jax.ShapeDtypeStruct((PAIRS, ROWS, LANES), f32),
            jax.ShapeDtypeStruct((ROWS, LANES), f32),
            jax.ShapeDtypeStruct((2, 2 * LEV, LANES), f32),
        ),
        in_specs=[anywhere] * 5,
        out_specs=(anywhere, whole, whole),
        scratch_shapes=[
            vmem((PAIRS + extra, ROWS, LANES), f32),
            vmem((PAIRS, ROWS, LANES), f32),
            vmem((SLOTS, GROUP, HALF, LANES), f32),
            vmem((SLOTS, 16, HALF, LANES), f32),
            vmem((SLOTS, 16, HALF, LANES), f32),
            vmem((2, 2, 8, 256, 256), jnp.bfloat16),
            vmem((2, 8, ROWS, 256), f32),
            vmem((2, ROWS), jnp.int32),
            vmem((8, 256), f32),
            vmem((2, ROWS, LANES), f32),
            vmem((2, 2, ROWS, LANES), f32),
            vmem((2, 2, 2 * LEV, LANES), f32),
            vmem((2, 2, 2 * LEV, LANES), f32),
            dma((SLOTS,)), dma((CHUNKS,)), dma((SLOTS,)), dma((SLOTS,)), dma((SLOTS,)), dma((SLOTS,)),
            dma((CHUNKS + SLOTS,)),
            dma((2, 2)), dma((2, 2)), dma((2, 2)), dma((2, 2)), dma((7,)),
        ],
        compiler_params=pltpu.CompilerParams(
            collective_id=0, has_side_effects=True, vmem_limit_bytes=48 << 20
        ),
        name="exchange_filter",
    )(
        adjoint_in.reshape(PAIRS, ROWS, LANES),
        trajectory.reshape(PAIRS, ROWS, LANES),
        cutoffs,
        jnp.asarray(INVERSE_K2),
        jnp.asarray(TABLES),
    )
    field = pl.BlockSpec((3, LEVELS_STEP, ROWS, LANES), lambda i: (0, i, 0, 0))
    return pl.pallas_call(
        stencil_kernel,
        grid=(LEV // LEVELS_STEP,),
        out_shape=jax.ShapeDtypeStruct((3, LEV, ROWS, LANES), f32),
        in_specs=[field, field, whole, whole],
        out_specs=field,
        compiler_params=pltpu.CompilerParams(vmem_limit_bytes=24 << 20),
        name="adjoint_stencil",
    )(trajectory, mu.reshape(3, LEV, ROWS, LANES), ew, ns)


def solution(mesh):
    in_specs = (P(None, None, "lat", "lon"), P(None, None, "lat", "lon"), P())
    out_specs = P(None, None, "lat", "lon")
    return jax.shard_map(
        per_device, mesh=mesh, in_specs=in_specs, out_specs=out_specs, check_vma=False
    )
```

```python
import functools

import jax
import jax.numpy as jnp
import ml_dtypes
import numpy as np
from jax import lax
from jax.experimental import pallas as pl
from jax.experimental.pallas import tpu as pltpu
from jax.sharding import PartitionSpec as P

MESH = pl.DeviceIdType.MESH
NLON, LEV, ROWS, LANES, LON, LAT = 2048, 32, 64, 128, 16, 8
PAIRS = 3 * LEV
GROUP, PIECE = 8, 32
PARTS = ROWS // PIECE
CHUNKS = PARTS * PAIRS // GROUP
HOME, SINGLE, FAR, NEAR = (8, 1, 1), (3, 1, 1), (3, 1, 1), (2, 1, 1)
KINDS = (HOME, SINGLE, FAR, NEAR)
SLOTS = max(sum(kind) for kind in KINDS)
AHEAD, LEAD, LAG = 8, 1, 2
cx, cy, cg, ca = 0.25, 0.25, 0.3, 0.25


def tables():
    m = np.arange(LANES)[:, None]
    k = np.arange(LANES)[None, :]
    forward = np.zeros((8, 256, 256))
    inverse = np.zeros((8, 256, 256))

    def angle(freq):
        return 2.0 * np.pi / NLON * ((freq * m) % NLON)

    for q in range(1, 8):
        freq = 16 * k + q
        cos, sin = np.cos(angle(freq)), np.sin(angle(freq))
        forward[q] = np.block([[cos, -sin], [sin, cos]])
        inverse[q] = forward[q].T / NLON
    index = np.arange(LANES)
    for at, q, is_cos, order in (
        (0, 0, index <= 64, np.where(index <= 64, index, index - 64)),
        (128, 8, index < 64, index % 64),
    ):
        freq = (16 * order + q)[None, :]
        block = np.where(is_cos[None, :], np.cos(angle(freq)), -np.sin(angle(freq)))
        weight = np.where((freq == 0) | (freq == NLON // 2), 1.0, 2.0)
        forward[0, at : at + 128, at : at + 128] = block
        inverse[0, at : at + 128, at : at + 128] = (block * weight).T / NLON
    both = np.stack([forward, inverse])
    high = both.astype(np.float32).astype(ml_dtypes.bfloat16)
    low = (both - high.astype(np.float64)).astype(np.float32).astype(ml_dtypes.bfloat16)
    return np.stack([high, low], 1)


def cadd(a, b, sign=1.0):
    re = a[0] + b[0] if sign > 0 else a[0] - b[0]
    if a[1] is None and b[1] is None:
        return (re, None)
    if a[1] is None:
        return (re, b[1] if sign > 0 else -b[1])
    if b[1] is None:
        return (re, a[1])
    return (re, a[1] + b[1] if sign > 0 else a[1] - b[1])


def conj(a):
    return a if a[1] is None else (a[0], -a[1])


def ctwist(a, k, n, sign):
    if k == 0:
        return a
    re, im = a
    if 4 * k == n:
        if im is None:
            return (jnp.zeros_like(re), re if sign > 0 else -re)
        return (-im, re) if sign > 0 else (im, -re)
    c, s = float(np.cos(2 * np.pi * k / n)), sign * float(np.sin(2 * np.pi * k / n))
    if im is None:
        return (re * c, re * s)
    if 8 * k == n:
        return ((re - im) * c, (re + im) * c) if sign > 0 else ((re + im) * c, (im - re) * c)
    return (re * c - im * s, re * s + im * c)


def real_dft(xs):
    n = len(xs)
    if n == 1:
        return [(xs[0], None)]
    if n == 2:
        return [(xs[0] + xs[1], None), (xs[0] - xs[1], None)]
    even, odd = real_dft(xs[0::2]), real_dft(xs[1::2])
    out = [None] * (n // 2 + 1)
    for k in range(n // 4 + 1):
        turned = ctwist(odd[k], k, n, -1)
        out[k] = cadd(even[k], turned)
        if k != n // 4:
            out[n // 2 - k] = conj(cadd(even[k], turned, -1.0))
    return out


def real_inverse(spec):
    n = 2 * (len(spec) - 1)
    if n == 2:
        return [spec[0][0] + spec[1][0], spec[0][0] - spec[1][0]]
    even, odd = [], []
    for k in range(n // 4 + 1):
        other = conj(spec[n // 2 - k])
        even.append(cadd(spec[k], other))
        odd.append(ctwist(cadd(spec[k], other, -1.0), k, n, 1))
    for part in (even, odd):
        part[0] = (part[0][0], None)
        part[-1] = (part[-1][0], None)
    a, b = real_inverse(even), real_inverse(odd)
    return [v for both in zip(a, b) for v in both]


def product(z, high, low):
    hi = z.astype(jnp.bfloat16)
    lo = (z - hi.astype(jnp.float32)).astype(jnp.bfloat16)
    rows = z.shape[0]
    main = jnp.dot(jnp.concatenate([hi, lo], 0), high, preferred_element_type=jnp.float32)
    rest = jnp.dot(hi, low, preferred_element_type=jnp.float32)
    return main[:rows] + main[rows:] + rest


def filter_chunk(blocks, table, damp_of):
    spec = real_dft(blocks)
    groups = [jnp.concatenate([spec[0][0], spec[8][0]], 1)]
    groups += [jnp.concatenate(spec[q], 1) for q in range(1, 8)]
    back = []
    for q in range(8):
        waves = product(groups[q], table[0, 0, q], table[0, 1, q]) * damp_of(q)
        back.append(product(waves, table[1, 0, q], table[1, 1, q]))
    spec = [(back[0][:, :LANES], None)]
    spec += [(back[q][:, :LANES], back[q][:, LANES:]) for q in range(1, 8)]
    spec += [(back[0][:, LANES:], None)]
    return real_inverse(spec)


def flip_bits(value, mask, width=4):
    out = 0
    for bit in range(width):
        own = (value // (1 << bit)) % 2
        out = out + (1 << bit) * ((1 - own) if (mask >> bit) & 1 else own)
    return out


def numbered(kind, index, side):
    plain, beside, rest = KINDS[kind]
    plains, besides, rests = (sum(k[i] for k in KINDS[:kind]) for i in range(3))
    base = 2 * CHUNKS // 3
    at_beside = base + PARTS * (besides + index - plain) + (1 - side) * (PARTS - 1)
    at = rests + index - plain - beside
    at_rest = base + PARTS * (at // (PARTS - 1)) + at % (PARTS - 1) + side
    return jnp.where(index < plain, plains + index, jnp.where(index < plain + beside, at_beside, at_rest))


def exchange_kernel(
    adj, traj, cuts_in, table_in,
    mu, trj, ew_out, ns_out,
    rpass, rin, rcv, yout, table, damp, cuts, ew_send, ew_recv, ns_send, ns_recv,
    rpass_sem, pass_sem, rin_sem, relay_sem, fs_sem, rcv_sem, bs_sem, ro_sem, mu_sem,
    ews_sem, ewr_sem, nss_sem, nsr_sem, local_sem,
):
    lon = lax.axis_index("lon")
    lat = lax.axis_index("lat")
    core, chip = lon % 2, lon // 2
    mirror = flip_bits(lon, 8)
    is_cap = (lat == 0) | (lat == LAT - 1)
    is_single = (lat == 2) | (lat == 5)
    is_far = (lat == 1) | (lat == 6)
    is_near = (lat == 3) | (lat == 4)
    over_y = is_single | is_far
    helps = is_single | is_far | is_near
    own_side = jnp.where((lat == 0) | (lat == 2) | (lat == 3) | (lat == 6), 0, 1)
    cap_lat = (LAT - 1) * own_side

    def by_kind(values):
        helper = jnp.where(is_far, values[2], values[3])
        return jnp.where(is_cap, values[0], jnp.where(is_single, values[1], helper))

    waves = by_kind([sum(kind) for kind in KINDS])

    def to(lon_at, lat_at):
        return {"lon": lon_at, "lat": lat_at}

    peers = [to(flip_bits(lon, k), lat) for k in range(1, 16)]
    peers += [to(lon, (lat + 1) % LAT), to(lon, (lat + LAT - 1) % LAT)]
    peers += [to(lon, flip_bits(lat, 2, 3)), to(lon, flip_bits(lat, 6, 3)), to(mirror, flip_bits(lat, 1, 3))]
    barrier = pltpu.get_barrier_semaphore()
    for peer in peers:
        pl.semaphore_signal(barrier, inc=1, device_id=peer, device_id_type=MESH)

    traj_copy = pltpu.make_async_copy(traj, trj, local_sem.at[1])
    mu_copy = pltpu.make_async_copy(adj, mu.at[pl.ds(0, PAIRS)], local_sem.at[2])
    small_copies = [
        pltpu.make_async_copy(cuts_in, cuts, local_sem.at[3]),
        pltpu.make_async_copy(table_in, table, local_sem.at[0]),
    ]

    def chunk_of(ref, chunk):
        pair = pl.multiple_of(GROUP * (chunk // PARTS), GROUP)
        row = pl.multiple_of(PIECE * (chunk % PARTS), PIECE)
        return ref.at[pl.ds(pair, GROUP), pl.ds(row, PIECE)]

    @pl.when(is_cap)
    def _():
        for s in range(sum(HOME)):
            pltpu.make_async_copy(chunk_of(adj, numbered(0, s, own_side)), rin.at[s], rin_sem.at[s]).start()

    traj_copy.start()
    for copy in small_copies:
        copy.start()

    @pl.when(jnp.logical_not(is_cap))
    def _():
        mu_copy.start()

    pl.semaphore_wait(barrier, len(peers))

    def relay(chunk, device, to_ref, to_sem, slot):
        pltpu.make_async_remote_copy(
            src_ref=chunk_of(adj, chunk), dst_ref=to_ref.at[slot],
            send_sem=relay_sem.at[chunk], recv_sem=to_sem.at[slot],
            device_id=device, device_id_type=MESH,
        ).start()

    def chunk_at(s):
        return by_kind([numbered(kind, s, own_side) for kind in range(4)])

    place = jnp.where(is_near, mirror, lon)

    def remote(src, dst, send_sem, recv_sem, member, member_lat):
        pltpu.make_async_remote_copy(
            src_ref=src, dst_ref=dst, send_sem=send_sem, recv_sem=recv_sem,
            device_id=to(member, member_lat), device_id_type=MESH,
        ).start()

    def forward(s):
        pltpu.make_async_copy(rin.at[s], rin.at[s], rin_sem.at[s]).wait()
        dst = rcv.at[s, place]
        for k in range(1, 8):
            owner = flip_bits(chip, k, 3)
            remote(rin.at[s, owner], dst, fs_sem.at[s], rcv_sem.at[s], 2 * owner + s % 2, lat)

        @pl.when(core == s % 2)
        def _():
            pltpu.make_async_copy(rin.at[s, chip], dst, rcv_sem.at[s]).start()

        @pl.when(core != s % 2)
        def _():
            remote(rin.at[s, chip], dst, fs_sem.at[s], rcv_sem.at[s], 2 * chip + 1 - core, lat)

    behind = CHUNKS

    def block(land):
        pair = GROUP * (land // PARTS) + chip
        return mu.at[pair, pl.ds(pl.multiple_of(PIECE * (land % PARTS), PIECE), PIECE)]

    def work(s):
        chunk = chunk_at(s)
        row = pl.multiple_of(PIECE * (chunk % PARTS), PIECE)
        pltpu.make_async_copy(rcv.at[s], rcv.at[s], rcv_sem.at[s]).wait()
        done = filter_chunk(
            [rcv[s, d] for d in range(16)], table, lambda q: damp[q, pl.ds(row, PIECE), :]
        )
        for d in range(16):
            yout[s, d] = done[d]
        relayed = jnp.where(over_y, behind + s, chunk)
        relay_lat = jnp.where(over_y, lat, cap_lat)
        for k in range(1, 16):
            member = flip_bits(lon, k)
            land, land_lat = (relayed, relay_lat) if k & 8 else (chunk, cap_lat)
            remote(yout.at[s, member], block(land), bs_sem.at[s], mu_sem.at[land], member, land_lat)

        @pl.when(is_cap)
        def _():
            pltpu.make_async_copy(yout.at[s, lon], block(chunk), mu_sem.at[chunk]).start()

        @pl.when(jnp.logical_not(is_cap))
        def _():
            remote(yout.at[s, lon], block(chunk), bs_sem.at[s], mu_sem.at[chunk], lon, cap_lat)

    def pass_on(s):
        pltpu.make_async_copy(rpass.at[s], rpass.at[s], rpass_sem.at[s]).wait()
        remote(rpass.at[s], rin.at[s], pass_sem.at[s], rin_sem.at[s], lon, flip_bits(lat, 2, 3))

    def half_of(ref, chunk):
        pair = pl.multiple_of(GROUP * (chunk // PARTS) + 4 * (1 - chip // 4), 4)
        row = pl.multiple_of(PIECE * (chunk % PARTS), PIECE)
        return ref.at[pl.ds(pair, 4), pl.ds(row, PIECE)]

    def deliver(s):
        chunk = chunk_at(s)
        part = half_of(mu, behind + s)
        pltpu.make_async_copy(part, part, mu_sem.at[behind + s]).wait()
        remote(part, half_of(mu, chunk), ro_sem.at[s], mu_sem.at[chunk], lon, cap_lat)

    @pl.when(is_cap)
    def _():
        targets = (
            (1, to(lon, flip_bits(lat, 2, 3)), rin, rin_sem),
            (2, to(lon, flip_bits(lat, 6, 3)), rin, rin_sem),
            (3, to(mirror, flip_bits(lat, 1, 3)), rpass, rpass_sem),
        )
        for s in range(max(sum(kind) for kind in KINDS[1:])):
            for kind, device, to_ref, to_sem in targets:
                if s < sum(KINDS[kind]):
                    relay(numbered(kind, s, own_side), device, to_ref, to_sem, s)

        @pl.loop(0, AHEAD)
        def _(s):
            forward(s)

    lane = lax.broadcasted_iota(jnp.int32, (ROWS, LANES), 1)

    def pack(ref, kind):
        def body(level, packed):
            for at, f in ((0, 0), (LANES // 2, 1)):
                target = at + 2 * level
                turned = pltpu.roll(ref[f * LEV + level], target, axis=1)
                packed = jnp.where((lane == target) | (lane == (target + LANES - 1) % LANES), turned, packed)
            return packed

        ew_send[kind] = lax.fori_loop(0, LEV, body, jnp.zeros((ROWS, LANES), jnp.float32))

    def pack_rows(ref, kind, side):
        at = (0, ROWS - 1)[side]
        for first, f in ((0, 0), (LEV, 2)):
            @pl.loop(0, LEV)
            def _(level):
                ns_send[kind, side, pl.ds(first + level, 1), :] = ref[f * LEV + level, at : at + 1, :]

    def ew_copies(kind):
        return [
            pltpu.make_async_remote_copy(
                src_ref=ew_send.at[kind], dst_ref=ew_recv.at[kind, 1 - side],
                send_sem=ews_sem.at[kind, side], recv_sem=ewr_sem.at[kind, 1 - side],
                device_id=to((lon + step) % LON, lat), device_id_type=MESH,
            )
            for side, step in ((0, LON - 1), (1, 1))
        ]

    def ns_copies(kind):
        return [
            pltpu.make_async_remote_copy(
                src_ref=ns_send.at[kind, side], dst_ref=ns_recv.at[kind, 1 - side],
                send_sem=nss_sem.at[kind, side], recv_sem=nsr_sem.at[kind, 1 - side],
                device_id=to(lon, (lat + step) % LAT), device_id_type=MESH,
            )
            for side, step in ((0, LAT - 1), (1, 1))
        ]

    inner = (lat > 0, lat < LAT - 1)

    def send_columns(ref, kind):
        pack(ref, kind)
        for copy in ew_copies(kind):
            copy.start()

    def send_rows(ref, kind):
        for side, copy in enumerate(ns_copies(kind)):
            @pl.when(inner[side])
            def _():
                pack_rows(ref, kind, side)
                copy.start()

    traj_copy.wait()
    send_columns(trj, 0)
    send_rows(trj, 0)

    @pl.when(jnp.logical_not(is_cap))
    def _():
        mu_copy.wait()
        send_columns(mu, 1)
        send_rows(mu, 1)

    row_at = lax.broadcasted_iota(jnp.int32, (ROWS, ROWS), 0)
    col_at = lax.broadcasted_iota(jnp.int32, (ROWS, ROWS), 1)
    for copy in small_copies:
        copy.wait()
    cut = jnp.where(own_side == 0, cuts[0:1, :], cuts[1:2, :]).astype(jnp.float32)
    column = jnp.sum(jnp.where(row_at == col_at, cut, 0.0), axis=1, keepdims=True)
    at = lax.broadcasted_iota(jnp.int32, (1, 2 * LANES), 1)
    half = at % LANES
    alone = jnp.where(at < LANES, 16 * jnp.where(half <= 64, half, half - 64), 16 * (half % 64) + 8)
    for q in range(8):
        freq = 16 * half + q
        wave = alone if q == 0 else jnp.minimum(freq, NLON - freq)
        damp[q] = jnp.minimum(1.0, (column / jnp.maximum(wave, 1).astype(jnp.float32)) ** 2)

    lag = jnp.where(is_cap, 0, jnp.where(over_y, LAG, LEAD))

    @pl.loop(0, jnp.where(waves > 0, waves + lag, 0))
    def _(t):
        passed = t + jnp.where(is_cap, AHEAD, 0)

        @pl.when(passed < waves)
        def _():
            forward(passed)

        @pl.when(is_far & (t < sum(NEAR)))
        def _():
            pass_on(t)

        s = t - jnp.where(is_cap, 0, LEAD)

        @pl.when((s >= 0) & (s < waves) & (s % 2 == core))
        def _():
            work(s)

        @pl.when(over_y & (t >= LAG))
        def _():
            deliver(t - LAG)

    def arrived(chunk):
        part = chunk_of(mu, chunk)
        pltpu.make_async_copy(part, part, mu_sem.at[chunk]).wait()

    early = 2 * CHUNKS // 3

    @pl.when(is_cap)
    def _():
        for chunk in range(early):
            arrived(chunk)
        send_columns(mu, 1)
        for group in range(LEV // GROUP):
            arrived(early + PARTS * group + (PARTS - 1) * (1 - own_side))
        send_rows(mu, 1)

    for kind in range(2):
        for copy in ew_copies(kind):
            copy.wait()
    even = lane % 2 == 0
    first_part = (lane < LANES // 2 - 1) | (lane == LANES - 1)

    def swapped(x):
        return pltpu.roll(x, LANES // 2, axis=1)

    def beyond(kind):
        return jnp.where(
            even, pltpu.roll(ew_recv[kind, 0], 1, axis=1), pltpu.roll(ew_recv[kind, 1], LANES - 1, axis=1)
        )

    state, state_out = ew_send[0], beyond(0)
    adjoint, adjoint_out = ew_send[1], beyond(1)
    p_in = jnp.where(first_part, adjoint, swapped(adjoint))
    p_out = jnp.where(first_part, adjoint_out, swapped(adjoint_out))
    q_out = jnp.where(first_part, swapped(adjoint_out), adjoint_out)
    term = (0.25 * cx) * (swapped(state) + swapped(state_out)) * (p_out - p_in)
    term = term + jnp.where(first_part, cg, ca * state_out) * q_out
    ew_out[...] = jnp.where(even, -term, term)

    for side in range(2):
        @pl.when(inner[side])
        def _():
            for kind in range(2):
                ns_copies(kind)[side].wait_send()
                whole = ns_recv.at[kind, side]
                pltpu.make_async_copy(whole, whole, nsr_sem.at[kind, side]).wait()
            H_in, V_in = ns_send[0, side, :LEV], ns_send[0, side, LEV:]
            H_out, V_out = ns_recv[0, side, :LEV], ns_recv[0, side, LEV:]
            p_diff = (0.25 * cy) * (ns_recv[1, side, :LEV] - ns_send[1, side, :LEV])
            r_out = ns_recv[1, side, LEV:]
            sign = 1.0 if side else -1.0
            ns_out[side, :LEV] = sign * ((V_in + V_out) * p_diff + cg * r_out)
            ns_out[side, LEV:] = sign * ((H_in + H_out) * p_diff + ca * V_out * r_out)

        @pl.when(jnp.logical_not(inner[side]))
        def _():
            ns_out[side] = jnp.zeros((2 * LEV, LANES), jnp.float32)

    @pl.when(is_cap)
    def _():
        for kind in (1, 2, 3):
            for s in range(sum(KINDS[kind])):
                chunk = numbered(kind, s, own_side)
                part = chunk_of(mu, chunk)
                pltpu.make_async_copy(part, part, relay_sem.at[chunk]).wait()

    @pl.when(is_far)
    def _():
        for s in range(sum(NEAR)):
            pltpu.make_async_copy(rpass.at[s], rpass.at[s], pass_sem.at[s]).wait()

    @pl.loop(0, waves)
    def _(s):
        most = rin.at[s, pl.ds(0, 7)]
        sent = rcv.at[s, pl.ds(0, 15)]

        @pl.when(core == s % 2)
        def _():
            pltpu.make_async_copy(most, most, fs_sem.at[s]).wait()

        @pl.when(core != s % 2)
        def _():
            pltpu.make_async_copy(rin.at[s], rin.at[s], fs_sem.at[s]).wait()

        @pl.when((core == s % 2) & is_cap)
        def _():
            pltpu.make_async_copy(sent, sent, bs_sem.at[s]).wait()

        @pl.when((core == s % 2) & helps)
        def _():
            pltpu.make_async_copy(rcv.at[s], rcv.at[s], bs_sem.at[s]).wait()

        @pl.when(over_y)
        def _():
            half = rin.at[s, pl.ds(0, 4)]
            pltpu.make_async_copy(half, half, ro_sem.at[s]).wait()

    @pl.when(is_cap)
    def _():
        for group in range(LEV // GROUP):
            for part in range(PARTS - 1):
                arrived(early + PARTS * group + part + own_side)


LEVELS_STEP = 8


def stencil_kernel(traj, mu, ew, ns, out):
    first = pl.program_id(0) * LEVELS_STEP
    row = lax.broadcasted_iota(jnp.int32, (ROWS, LANES), 0)
    lane = lax.broadcasted_iota(jnp.int32, (ROWS, LANES), 1)
    edge = (lane == 0) | (lane == LANES - 1)

    def fluxes(p, a, b, r, axis):
        size = (ROWS, LANES)[axis]
        last = (row, lane)[axis] == size - 1

        def after(x):
            return pltpu.roll(x, size - 1, axis=axis)

        a_after = after(a)
        slope = jnp.where(last, 0.0, (0.25 * cx) * (after(p) - p))
        r_after = jnp.where(last, 0.0, after(r))
        r_here = jnp.where(last, 0.0, r)
        flux_h = (a + a_after) * slope
        flux_r = (b + after(b)) * slope
        to_h = (flux_h + cg * r_after) + pltpu.roll(flux_h - cg * r_here, 1, axis=axis)
        to_r = (flux_r + ca * (a_after * r_after)) + pltpu.roll(flux_r - ca * (a * r_here), 1, axis=axis)
        return to_h, to_r

    for j in range(LEVELS_STEP):
        level = first + j
        H, U, V = (traj[f * LEV + level] for f in range(3))
        p, q, r = (mu[f * LEV + level] for f in range(3))
        x_h, x_u = fluxes(p, U, H, q, 1)
        y_h, y_v = fluxes(p, V, H, r, 0)
        over_h = jnp.where(edge, pltpu.roll(ew[...], (LANES - 2 * level) % LANES, axis=1), 0.0)
        over_u = jnp.where(edge, pltpu.roll(ew[...], (LANES + LANES // 2 - 2 * level) % LANES, axis=1), 0.0)
        out[0, j] = p + x_h + y_h + over_h
        out[1, j] = q + x_u + over_u
        out[2, j] = r + y_v
        for side, at in ((0, 0), (1, ROWS - 1)):
            out[0, j, at : at + 1, :] += ns[side, pl.ds(level, 1), :]
            out[2, j, at : at + 1, :] += ns[side, pl.ds(LEV + level, 1), :]


TABLES = tables()


def per_device(trajectory, adjoint_in, cutoffs):
    f32 = jnp.float32
    whole = pl.BlockSpec(memory_space=pltpu.VMEM)
    anywhere = pl.BlockSpec(memory_space=pl.ANY)
    vmem = pltpu.VMEM
    dma = pltpu.SemaphoreType.DMA
    extra = GROUP * ((max(sum(SINGLE), sum(FAR)) + PARTS - 1) // PARTS)
    mu, trj, ew, ns = pl.pallas_call(
        exchange_kernel,
        out_shape=(
            vmem((PAIRS + extra, ROWS, LANES), f32),
            vmem((PAIRS, ROWS, LANES), f32),
            vmem((ROWS, LANES), f32),
            vmem((2, 2 * LEV, LANES), f32),
        ),
        in_specs=[anywhere] * 4,
        out_specs=(whole,) * 4,
        scratch_shapes=[
            vmem((sum(NEAR), GROUP, PIECE, LANES), f32),
            vmem((SLOTS, GROUP, PIECE, LANES), f32),
            vmem((SLOTS, 16, PIECE, LANES), f32),
            vmem((SLOTS, 16, PIECE, LANES), f32),
            vmem((2, 2, 8, 256, 256), jnp.bfloat16),
            vmem((8, ROWS, 256), f32),
            vmem((2, ROWS), jnp.int32),
            vmem((2, ROWS, LANES), f32),
            vmem((2, 2, ROWS, LANES), f32),
            vmem((2, 2, 2 * LEV, LANES), f32),
            vmem((2, 2, 2 * LEV, LANES), f32),
            dma((sum(NEAR),)), dma((sum(NEAR),)),
            dma((SLOTS,)), dma((CHUNKS,)), dma((SLOTS,)), dma((SLOTS,)), dma((SLOTS,)), dma((SLOTS,)),
            dma((CHUNKS + SLOTS,)),
            dma((2, 2)), dma((2, 2)), dma((2, 2)), dma((2, 2)), dma((4,)),
        ],
        compiler_params=pltpu.CompilerParams(
            collective_id=0, has_side_effects=True, vmem_limit_bytes=32 << 20
        ),
        name="exchange_filter",
    )(*(
        pltpu.with_memory_space_constraint(x, pltpu.HBM)
        for x in (
            adjoint_in.reshape(PAIRS, ROWS, LANES),
            trajectory.reshape(PAIRS, ROWS, LANES),
            cutoffs,
            jnp.asarray(TABLES),
        )
    ))
    return pl.pallas_call(
        stencil_kernel,
        grid=(LEV // LEVELS_STEP,),
        out_shape=jax.ShapeDtypeStruct((3, LEV, ROWS, LANES), f32),
        in_specs=[whole] * 4,
        out_specs=pl.BlockSpec((3, LEVELS_STEP, ROWS, LANES), lambda i: (0, i, 0, 0)),
        compiler_params=pltpu.CompilerParams(vmem_limit_bytes=24 << 20),
        name="adjoint_stencil",
    )(*(pltpu.with_memory_space_constraint(x, pltpu.VMEM) for x in (trj, mu, ew, ns)))


def solution(mesh):
    in_specs = (P(None, None, "lat", "lon"), P(None, None, "lat", "lon"), P())
    out_specs = P(None, None, "lat", "lon")
    return jax.shard_map(
        per_device, mesh=mesh, in_specs=in_specs, out_specs=out_specs, check_vma=False
    )
```

```python
import functools

import jax
import jax.numpy as jnp
import ml_dtypes
import numpy as np
from jax import lax
from jax.experimental import pallas as pl
from jax.experimental.pallas import tpu as pltpu
from jax.sharding import PartitionSpec as P

MESH = pl.DeviceIdType.MESH
NLON, LEV, ROWS, LANES, LON, LAT = 2048, 32, 64, 128, 16, 8
PAIRS = 3 * LEV
GROUP, PIECE = 8, 32
PARTS = ROWS // PIECE
CHUNKS = PARTS * PAIRS // GROUP
HOME, SINGLE, FAR, NEAR = (8, 1, 1), (3, 1, 1), (3, 1, 1), (2, 1, 1)
KINDS = (HOME, SINGLE, FAR, NEAR)
SLOTS = max(sum(kind) for kind in KINDS)
AHEAD, LEAD, LAG = 8, 1, 2
WINDOW = 1
cx, cy, cg, ca = 0.25, 0.25, 0.3, 0.25


def tables():
    m = np.arange(LANES)[:, None]
    k = np.arange(LANES)[None, :]
    forward = np.zeros((8, 256, 256))
    inverse = np.zeros((8, 256, 256))

    def angle(freq):
        return 2.0 * np.pi / NLON * ((freq * m) % NLON)

    for q in range(1, 8):
        freq = 16 * k + q
        cos, sin = np.cos(angle(freq)), np.sin(angle(freq))
        forward[q] = np.block([[cos, -sin], [sin, cos]])
        inverse[q] = forward[q].T / NLON
    index = np.arange(LANES)
    for at, q, is_cos, order in (
        (0, 0, index <= 64, np.where(index <= 64, index, index - 64)),
        (128, 8, index < 64, index % 64),
    ):
        freq = (16 * order + q)[None, :]
        block = np.where(is_cos[None, :], np.cos(angle(freq)), -np.sin(angle(freq)))
        weight = np.where((freq == 0) | (freq == NLON // 2), 1.0, 2.0)
        forward[0, at : at + 128, at : at + 128] = block
        inverse[0, at : at + 128, at : at + 128] = (block * weight).T / NLON
    both = np.stack([forward, inverse])
    high = both.astype(np.float32).astype(ml_dtypes.bfloat16)
    low = (both - high.astype(np.float64)).astype(np.float32).astype(ml_dtypes.bfloat16)
    return np.stack([high, low], 1)


def cadd(a, b, sign=1.0):
    re = a[0] + b[0] if sign > 0 else a[0] - b[0]
    if a[1] is None and b[1] is None:
        return (re, None)
    if a[1] is None:
        return (re, b[1] if sign > 0 else -b[1])
    if b[1] is None:
        return (re, a[1])
    return (re, a[1] + b[1] if sign > 0 else a[1] - b[1])


def conj(a):
    return a if a[1] is None else (a[0], -a[1])


def ctwist(a, k, n, sign):
    if k == 0:
        return a
    re, im = a
    if 4 * k == n:
        if im is None:
            return (jnp.zeros_like(re), re if sign > 0 else -re)
        return (-im, re) if sign > 0 else (im, -re)
    c, s = float(np.cos(2 * np.pi * k / n)), sign * float(np.sin(2 * np.pi * k / n))
    if im is None:
        return (re * c, re * s)
    if 8 * k == n:
        return ((re - im) * c, (re + im) * c) if sign > 0 else ((re + im) * c, (im - re) * c)
    return (re * c - im * s, re * s + im * c)


def real_dft(xs):
    n = len(xs)
    if n == 1:
        return [(xs[0], None)]
    if n == 2:
        return [(xs[0] + xs[1], None), (xs[0] - xs[1], None)]
    even, odd = real_dft(xs[0::2]), real_dft(xs[1::2])
    out = [None] * (n // 2 + 1)
    for k in range(n // 4 + 1):
        turned = ctwist(odd[k], k, n, -1)
        out[k] = cadd(even[k], turned)
        if k != n // 4:
            out[n // 2 - k] = conj(cadd(even[k], turned, -1.0))
    return out


def real_inverse(spec):
    n = 2 * (len(spec) - 1)
    if n == 2:
        return [spec[0][0] + spec[1][0], spec[0][0] - spec[1][0]]
    even, odd = [], []
    for k in range(n // 4 + 1):
        other = conj(spec[n // 2 - k])
        even.append(cadd(spec[k], other))
        odd.append(ctwist(cadd(spec[k], other, -1.0), k, n, 1))
    for part in (even, odd):
        part[0] = (part[0][0], None)
        part[-1] = (part[-1][0], None)
    a, b = real_inverse(even), real_inverse(odd)
    return [v for both in zip(a, b) for v in both]


def product(z, high, low):
    hi = z.astype(jnp.bfloat16)
    lo = (z - hi.astype(jnp.float32)).astype(jnp.bfloat16)
    rows = z.shape[0]
    main = jnp.dot(jnp.concatenate([hi, lo], 0), high, preferred_element_type=jnp.float32)
    rest = jnp.dot(hi, low, preferred_element_type=jnp.float32)
    return main[:rows] + main[rows:] + rest


def filter_chunk(blocks, table, damp_of):
    spec = real_dft(blocks)
    groups = [jnp.concatenate([spec[0][0], spec[8][0]], 1)]
    groups += [jnp.concatenate(spec[q], 1) for q in range(1, 8)]
    back = []
    for q in range(8):
        waves = product(groups[q], table[0, 0, q], table[0, 1, q]) * damp_of(q)
        back.append(product(waves, table[1, 0, q], table[1, 1, q]))
    spec = [(back[0][:, :LANES], None)]
    spec += [(back[q][:, :LANES], back[q][:, LANES:]) for q in range(1, 8)]
    spec += [(back[0][:, LANES:], None)]
    return real_inverse(spec)


def flip_bits(value, mask, width=4):
    out = 0
    for bit in range(width):
        own = (value // (1 << bit)) % 2
        out = out + (1 << bit) * ((1 - own) if (mask >> bit) & 1 else own)
    return out


def numbered(kind, index, side):
    plain, beside, rest = KINDS[kind]
    plains, besides, rests = (sum(k[i] for k in KINDS[:kind]) for i in range(3))
    base = 2 * CHUNKS // 3
    at_beside = base + PARTS * (besides + index - plain) + (1 - side) * (PARTS - 1)
    at = rests + index - plain - beside
    at_rest = base + PARTS * (at // (PARTS - 1)) + at % (PARTS - 1) + side
    return jnp.where(index < plain, plains + index, jnp.where(index < plain + beside, at_beside, at_rest))


def exchange_kernel(
    adj, traj, cuts_in, table_in,
    mu, trj, ew_out, ns_out,
    rpass, rin, rcv, yout, table, damp, cuts, ew_send, ew_recv, ns_send, ns_recv,
    rpass_sem, pass_sem, rin_sem, relay_sem, fs_sem, rcv_sem, bs_sem, ro_sem, mu_sem,
    ews_sem, ewr_sem, nss_sem, nsr_sem, local_sem,
):
    lon = lax.axis_index("lon")
    lat = lax.axis_index("lat")
    core, chip = lon % 2, lon // 2
    mirror = flip_bits(lon, 8)
    is_cap = (lat == 0) | (lat == LAT - 1)
    is_single = (lat == 2) | (lat == 5)
    is_far = (lat == 1) | (lat == 6)
    is_near = (lat == 3) | (lat == 4)
    over_y = is_single | is_far
    helps = is_single | is_far | is_near
    own_side = jnp.where((lat == 0) | (lat == 2) | (lat == 3) | (lat == 6), 0, 1)
    cap_lat = (LAT - 1) * own_side

    def by_kind(values):
        helper = jnp.where(is_far, values[2], values[3])
        return jnp.where(is_cap, values[0], jnp.where(is_single, values[1], helper))

    waves = by_kind([sum(kind) for kind in KINDS])

    def to(lon_at, lat_at):
        return {"lon": lon_at, "lat": lat_at}

    peers = [to(flip_bits(lon, k), lat) for k in range(1, 16)]
    peers += [to(lon, (lat + 1) % LAT), to(lon, (lat + LAT - 1) % LAT)]
    peers += [to(lon, flip_bits(lat, 2, 3)), to(lon, flip_bits(lat, 6, 3)), to(mirror, flip_bits(lat, 1, 3))]
    barrier = pltpu.get_barrier_semaphore()
    for peer in peers:
        pl.semaphore_signal(barrier, inc=1, device_id=peer, device_id_type=MESH)

    traj_copy = pltpu.make_async_copy(traj, trj, local_sem.at[1])
    mu_copy = pltpu.make_async_copy(adj, mu.at[pl.ds(0, PAIRS)], local_sem.at[2])
    small_copies = [
        pltpu.make_async_copy(cuts_in, cuts, local_sem.at[3]),
        pltpu.make_async_copy(table_in, table, local_sem.at[0]),
    ]

    def chunk_of(ref, chunk):
        pair = pl.multiple_of(GROUP * (chunk // PARTS), GROUP)
        row = pl.multiple_of(PIECE * (chunk % PARTS), PIECE)
        return ref.at[pl.ds(pair, GROUP), pl.ds(row, PIECE)]

    @pl.when(is_cap)
    def _():
        for s in range(sum(HOME)):
            pltpu.make_async_copy(chunk_of(adj, numbered(0, s, own_side)), rin.at[s], rin_sem.at[s]).start()

    traj_copy.start()
    for copy in small_copies:
        copy.start()

    @pl.when(jnp.logical_not(is_cap))
    def _():
        mu_copy.start()

    pl.semaphore_wait(barrier, len(peers))

    targets = {
        1: (to(lon, flip_bits(lat, 2, 3)), rin, rin_sem),
        2: (to(lon, flip_bits(lat, 6, 3)), rin, rin_sem),
        3: (to(mirror, flip_bits(lat, 1, 3)), rpass, rpass_sem),
    }

    def relay(kind, s):
        device, to_ref, to_sem = targets[kind]
        chunk = numbered(kind, s, own_side)
        pltpu.make_async_remote_copy(
            src_ref=chunk_of(adj, chunk), dst_ref=to_ref.at[s],
            send_sem=relay_sem.at[chunk], recv_sem=to_sem.at[s],
            device_id=device, device_id_type=MESH,
        ).start()

    def relayed_out(kind, s):
        chunk = numbered(kind, s, own_side)
        part = chunk_of(mu, chunk)
        pltpu.make_async_copy(part, part, relay_sem.at[chunk]).wait()

    def chunk_at(s):
        return by_kind([numbered(kind, s, own_side) for kind in range(4)])

    place = jnp.where(is_near, mirror, lon)

    def remote(src, dst, send_sem, recv_sem, member, member_lat):
        pltpu.make_async_remote_copy(
            src_ref=src, dst_ref=dst, send_sem=send_sem, recv_sem=recv_sem,
            device_id=to(member, member_lat), device_id_type=MESH,
        ).start()

    def forward(s):
        pltpu.make_async_copy(rin.at[s], rin.at[s], rin_sem.at[s]).wait()
        dst = rcv.at[s, place]
        for k in range(1, 8):
            owner = flip_bits(chip, k, 3)
            remote(rin.at[s, owner], dst, fs_sem.at[s], rcv_sem.at[s], 2 * owner + s % 2, lat)

        @pl.when(core == s % 2)
        def _():
            pltpu.make_async_copy(rin.at[s, chip], dst, rcv_sem.at[s]).start()

        @pl.when(core != s % 2)
        def _():
            remote(rin.at[s, chip], dst, fs_sem.at[s], rcv_sem.at[s], 2 * chip + 1 - core, lat)

    behind = CHUNKS

    def block(land):
        pair = GROUP * (land // PARTS) + chip
        return mu.at[pair, pl.ds(pl.multiple_of(PIECE * (land % PARTS), PIECE), PIECE)]

    def work(s):
        chunk = chunk_at(s)
        row = pl.multiple_of(PIECE * (chunk % PARTS), PIECE)
        pltpu.make_async_copy(rcv.at[s], rcv.at[s], rcv_sem.at[s]).wait()
        done = filter_chunk(
            [rcv[s, d] for d in range(16)], table, lambda q: damp[q, pl.ds(row, PIECE), :]
        )
        for d in range(16):
            yout[s, d] = done[d]
        relayed = jnp.where(over_y, behind + s, chunk)
        relay_lat = jnp.where(over_y, lat, cap_lat)
        for k in range(1, 16):
            member = flip_bits(lon, k)
            land, land_lat = (relayed, relay_lat) if k & 8 else (chunk, cap_lat)
            remote(yout.at[s, member], block(land), bs_sem.at[s], mu_sem.at[land], member, land_lat)

        @pl.when(is_cap)
        def _():
            pltpu.make_async_copy(yout.at[s, lon], block(chunk), mu_sem.at[chunk]).start()

        @pl.when(jnp.logical_not(is_cap))
        def _():
            remote(yout.at[s, lon], block(chunk), bs_sem.at[s], mu_sem.at[chunk], lon, cap_lat)

    def pass_on(s):
        pltpu.make_async_copy(rpass.at[s], rpass.at[s], rpass_sem.at[s]).wait()
        remote(rpass.at[s], rin.at[s], pass_sem.at[s], rin_sem.at[s], lon, flip_bits(lat, 2, 3))

    def half_of(ref, chunk):
        pair = pl.multiple_of(GROUP * (chunk // PARTS) + 4 * (1 - chip // 4), 4)
        row = pl.multiple_of(PIECE * (chunk % PARTS), PIECE)
        return ref.at[pl.ds(pair, 4), pl.ds(row, PIECE)]

    def deliver(s):
        chunk = chunk_at(s)
        part = half_of(mu, behind + s)
        pltpu.make_async_copy(part, part, mu_sem.at[behind + s]).wait()
        remote(part, half_of(mu, chunk), ro_sem.at[s], mu_sem.at[chunk], lon, cap_lat)

    @pl.when(is_cap)
    def _():
        for s in range(WINDOW):
            for kind in (1, 2, 3):
                if s < sum(KINDS[kind]):
                    relay(kind, s)

        @pl.loop(0, AHEAD)
        def _(s):
            forward(s)

    lane = lax.broadcasted_iota(jnp.int32, (ROWS, LANES), 1)

    def pack(ref, kind):
        def body(level, packed):
            for at, f in ((0, 0), (LANES // 2, 1)):
                target = at + 2 * level
                turned = pltpu.roll(ref[f * LEV + level], target, axis=1)
                packed = jnp.where((lane == target) | (lane == (target + LANES - 1) % LANES), turned, packed)
            return packed

        ew_send[kind] = lax.fori_loop(0, LEV, body, jnp.zeros((ROWS, LANES), jnp.float32))

    def pack_rows(ref, kind, side):
        at = (0, ROWS - 1)[side]
        for first, f in ((0, 0), (LEV, 2)):
            @pl.loop(0, LEV)
            def _(level):
                ns_send[kind, side, pl.ds(first + level, 1), :] = ref[f * LEV + level, at : at + 1, :]

    def ew_copies(kind):
        return [
            pltpu.make_async_remote_copy(
                src_ref=ew_send.at[kind], dst_ref=ew_recv.at[kind, 1 - side],
                send_sem=ews_sem.at[kind, side], recv_sem=ewr_sem.at[kind, 1 - side],
                device_id=to((lon + step) % LON, lat), device_id_type=MESH,
            )
            for side, step in ((0, LON - 1), (1, 1))
        ]

    def ns_copies(kind):
        return [
            pltpu.make_async_remote_copy(
                src_ref=ns_send.at[kind, side], dst_ref=ns_recv.at[kind, 1 - side],
                send_sem=nss_sem.at[kind, side], recv_sem=nsr_sem.at[kind, 1 - side],
                device_id=to(lon, (lat + step) % LAT), device_id_type=MESH,
            )
            for side, step in ((0, LAT - 1), (1, 1))
        ]

    inner = (lat > 0, lat < LAT - 1)

    def send_columns(ref, kind):
        pack(ref, kind)
        for copy in ew_copies(kind):
            copy.start()

    def send_rows(ref, kind):
        for side, copy in enumerate(ns_copies(kind)):
            @pl.when(inner[side])
            def _():
                pack_rows(ref, kind, side)
                copy.start()

    traj_copy.wait()
    send_columns(trj, 0)
    send_rows(trj, 0)

    @pl.when(jnp.logical_not(is_cap))
    def _():
        mu_copy.wait()
        send_columns(mu, 1)
        send_rows(mu, 1)

    row_at = lax.broadcasted_iota(jnp.int32, (ROWS, ROWS), 0)
    col_at = lax.broadcasted_iota(jnp.int32, (ROWS, ROWS), 1)
    for copy in small_copies:
        copy.wait()
    cut = jnp.where(own_side == 0, cuts[0:1, :], cuts[1:2, :]).astype(jnp.float32)
    column = jnp.sum(jnp.where(row_at == col_at, cut, 0.0), axis=1, keepdims=True)
    at = lax.broadcasted_iota(jnp.int32, (1, 2 * LANES), 1)
    half = at % LANES
    alone = jnp.where(at < LANES, 16 * jnp.where(half <= 64, half, half - 64), 16 * (half % 64) + 8)
    for q in range(8):
        freq = 16 * half + q
        wave = alone if q == 0 else jnp.minimum(freq, NLON - freq)
        damp[q] = jnp.minimum(1.0, (column / jnp.maximum(wave, 1).astype(jnp.float32)) ** 2)

    lag = jnp.where(is_cap, 0, jnp.where(over_y, LAG, LEAD))

    @pl.loop(0, jnp.where(waves > 0, waves + lag, 0))
    def _(t):
        for kind in (1, 2, 3):
            @pl.when(is_cap & (t < sum(KINDS[kind]) - WINDOW))
            def _():
                relayed_out(kind, t)
                relay(kind, t + WINDOW)

        passed = t + jnp.where(is_cap, AHEAD, 0)

        @pl.when(passed < waves)
        def _():
            forward(passed)

        s = t - jnp.where(is_cap, 0, LEAD)

        @pl.when((s >= 0) & (s < waves) & (s % 2 == core))
        def _():
            work(s)

        @pl.when(is_far & (t < sum(NEAR)))
        def _():
            pass_on(t)

        @pl.when(over_y & (t >= LAG))
        def _():
            deliver(t - LAG)

    def arrived(chunk):
        part = chunk_of(mu, chunk)
        pltpu.make_async_copy(part, part, mu_sem.at[chunk]).wait()

    early = 2 * CHUNKS // 3

    @pl.when(is_cap)
    def _():
        for chunk in range(early):
            arrived(chunk)
        send_columns(mu, 1)
        for group in range(LEV // GROUP):
            arrived(early + PARTS * group + (PARTS - 1) * (1 - own_side))
        send_rows(mu, 1)

    for kind in range(2):
        for copy in ew_copies(kind):
            copy.wait()
    even = lane % 2 == 0
    first_part = (lane < LANES // 2 - 1) | (lane == LANES - 1)

    def swapped(x):
        return pltpu.roll(x, LANES // 2, axis=1)

    def beyond(kind):
        return jnp.where(
            even, pltpu.roll(ew_recv[kind, 0], 1, axis=1), pltpu.roll(ew_recv[kind, 1], LANES - 1, axis=1)
        )

    state, state_out = ew_send[0], beyond(0)
    adjoint, adjoint_out = ew_send[1], beyond(1)
    p_in = jnp.where(first_part, adjoint, swapped(adjoint))
    p_out = jnp.where(first_part, adjoint_out, swapped(adjoint_out))
    q_out = jnp.where(first_part, swapped(adjoint_out), adjoint_out)
    term = (0.25 * cx) * (swapped(state) + swapped(state_out)) * (p_out - p_in)
    term = term + jnp.where(first_part, cg, ca * state_out) * q_out
    ew_out[...] = jnp.where(even, -term, term)

    for side in range(2):
        @pl.when(inner[side])
        def _():
            for kind in range(2):
                ns_copies(kind)[side].wait_send()
                whole = ns_recv.at[kind, side]
                pltpu.make_async_copy(whole, whole, nsr_sem.at[kind, side]).wait()
            H_in, V_in = ns_send[0, side, :LEV], ns_send[0, side, LEV:]
            H_out, V_out = ns_recv[0, side, :LEV], ns_recv[0, side, LEV:]
            p_diff = (0.25 * cy) * (ns_recv[1, side, :LEV] - ns_send[1, side, :LEV])
            r_out = ns_recv[1, side, LEV:]
            sign = 1.0 if side else -1.0
            ns_out[side, :LEV] = sign * ((V_in + V_out) * p_diff + cg * r_out)
            ns_out[side, LEV:] = sign * ((H_in + H_out) * p_diff + ca * V_out * r_out)

        @pl.when(jnp.logical_not(inner[side]))
        def _():
            ns_out[side] = jnp.zeros((2 * LEV, LANES), jnp.float32)

    @pl.when(is_cap)
    def _():
        for kind in (1, 2, 3):
            for s in range(max(sum(KINDS[kind]) - WINDOW, 0), sum(KINDS[kind])):
                relayed_out(kind, s)

    @pl.when(is_far)
    def _():
        for s in range(sum(NEAR)):
            pltpu.make_async_copy(rpass.at[s], rpass.at[s], pass_sem.at[s]).wait()

    @pl.loop(0, waves)
    def _(s):
        most = rin.at[s, pl.ds(0, 7)]
        sent = rcv.at[s, pl.ds(0, 15)]

        @pl.when(core == s % 2)
        def _():
            pltpu.make_async_copy(most, most, fs_sem.at[s]).wait()

        @pl.when(core != s % 2)
        def _():
            pltpu.make_async_copy(rin.at[s], rin.at[s], fs_sem.at[s]).wait()

        @pl.when((core == s % 2) & is_cap)
        def _():
            pltpu.make_async_copy(sent, sent, bs_sem.at[s]).wait()

        @pl.when((core == s % 2) & helps)
        def _():
            pltpu.make_async_copy(rcv.at[s], rcv.at[s], bs_sem.at[s]).wait()

        @pl.when(over_y)
        def _():
            half = rin.at[s, pl.ds(0, 4)]
            pltpu.make_async_copy(half, half, ro_sem.at[s]).wait()

    @pl.when(is_cap)
    def _():
        for group in range(LEV // GROUP):
            for part in range(PARTS - 1):
                arrived(early + PARTS * group + part + own_side)


LEVELS_STEP = 8


def stencil_kernel(traj, mu, ew, ns, out):
    first = pl.program_id(0) * LEVELS_STEP
    row = lax.broadcasted_iota(jnp.int32, (ROWS, LANES), 0)
    lane = lax.broadcasted_iota(jnp.int32, (ROWS, LANES), 1)
    edge = (lane == 0) | (lane == LANES - 1)

    def fluxes(p, a, b, r, axis):
        size = (ROWS, LANES)[axis]
        last = (row, lane)[axis] == size - 1

        def after(x):
            return pltpu.roll(x, size - 1, axis=axis)

        a_after = after(a)
        slope = jnp.where(last, 0.0, (0.25 * cx) * (after(p) - p))
        r_after = jnp.where(last, 0.0, after(r))
        r_here = jnp.where(last, 0.0, r)
        flux_h = (a + a_after) * slope
        flux_r = (b + after(b)) * slope
        to_h = (flux_h + cg * r_after) + pltpu.roll(flux_h - cg * r_here, 1, axis=axis)
        to_r = (flux_r + ca * (a_after * r_after)) + pltpu.roll(flux_r - ca * (a * r_here), 1, axis=axis)
        return to_h, to_r

    for j in range(LEVELS_STEP):
        level = first + j
        H, U, V = (traj[f * LEV + level] for f in range(3))
        p, q, r = (mu[f * LEV + level] for f in range(3))
        x_h, x_u = fluxes(p, U, H, q, 1)
        y_h, y_v = fluxes(p, V, H, r, 0)
        over_h = jnp.where(edge, pltpu.roll(ew[...], (LANES - 2 * level) % LANES, axis=1), 0.0)
        over_u = jnp.where(edge, pltpu.roll(ew[...], (LANES + LANES // 2 - 2 * level) % LANES, axis=1), 0.0)
        out[0, j] = p + x_h + y_h + over_h
        out[1, j] = q + x_u + over_u
        out[2, j] = r + y_v
        for side, at in ((0, 0), (1, ROWS - 1)):
            out[0, j, at : at + 1, :] += ns[side, pl.ds(level, 1), :]
            out[2, j, at : at + 1, :] += ns[side, pl.ds(LEV + level, 1), :]


TABLES = tables()


def per_device(trajectory, adjoint_in, cutoffs):
    f32 = jnp.float32
    whole = pl.BlockSpec(memory_space=pltpu.VMEM)
    anywhere = pl.BlockSpec(memory_space=pl.ANY)
    vmem = pltpu.VMEM
    dma = pltpu.SemaphoreType.DMA
    extra = GROUP * ((max(sum(SINGLE), sum(FAR)) + PARTS - 1) // PARTS)
    mu, trj, ew, ns = pl.pallas_call(
        exchange_kernel,
        out_shape=(
            vmem((PAIRS + extra, ROWS, LANES), f32),
            vmem((PAIRS, ROWS, LANES), f32),
            vmem((ROWS, LANES), f32),
            vmem((2, 2 * LEV, LANES), f32),
        ),
        in_specs=[anywhere] * 4,
        out_specs=(whole,) * 4,
        scratch_shapes=[
            vmem((sum(NEAR), GROUP, PIECE, LANES), f32),
            vmem((SLOTS, GROUP, PIECE, LANES), f32),
            vmem((SLOTS, 16, PIECE, LANES), f32),
            vmem((SLOTS, 16, PIECE, LANES), f32),
            vmem((2, 2, 8, 256, 256), jnp.bfloat16),
            vmem((8, ROWS, 256), f32),
            vmem((2, ROWS), jnp.int32),
            vmem((2, ROWS, LANES), f32),
            vmem((2, 2, ROWS, LANES), f32),
            vmem((2, 2, 2 * LEV, LANES), f32),
            vmem((2, 2, 2 * LEV, LANES), f32),
            dma((sum(NEAR),)), dma((sum(NEAR),)),
            dma((SLOTS,)), dma((CHUNKS,)), dma((SLOTS,)), dma((SLOTS,)), dma((SLOTS,)), dma((SLOTS,)),
            dma((CHUNKS + SLOTS,)),
            dma((2, 2)), dma((2, 2)), dma((2, 2)), dma((2, 2)), dma((4,)),
        ],
        compiler_params=pltpu.CompilerParams(
            collective_id=0, has_side_effects=True, vmem_limit_bytes=32 << 20
        ),
        name="exchange_filter",
    )(*(
        pltpu.with_memory_space_constraint(x, pltpu.HBM)
        for x in (
            adjoint_in.reshape(PAIRS, ROWS, LANES),
            trajectory.reshape(PAIRS, ROWS, LANES),
            cutoffs,
            jnp.asarray(TABLES),
        )
    ))
    return pl.pallas_call(
        stencil_kernel,
        grid=(LEV // LEVELS_STEP,),
        out_shape=jax.ShapeDtypeStruct((3, LEV, ROWS, LANES), f32),
        in_specs=[whole] * 4,
        out_specs=pl.BlockSpec((3, LEVELS_STEP, ROWS, LANES), lambda i: (0, i, 0, 0)),
        compiler_params=pltpu.CompilerParams(vmem_limit_bytes=24 << 20),
        name="adjoint_stencil",
    )(*(pltpu.with_memory_space_constraint(x, pltpu.VMEM) for x in (trj, mu, ew, ns)))


def solution(mesh):
    in_specs = (P(None, None, "lat", "lon"), P(None, None, "lat", "lon"), P())
    out_specs = P(None, None, "lat", "lon")
    return jax.shard_map(
        per_device, mesh=mesh, in_specs=in_specs, out_specs=out_specs, check_vma=False
    )
```
